512 devices in a mesh: ctx: 128 (over x_hi, y, z), exp: 4 (over x_lo, core).
Axes of the slice: x: 4 (x_hi: 2, x_lo: 2; x = x_hi * 2 + x_lo), y: 8, z: 8, core: 2. Of those that a mesh axis runs over, the one named last changes fastest.
Arguments:
- hidden_state_stream: bfloat16 [32768, 2048], P('ctx', 'exp'), may hold values from -6 to 6
- question_vectors: bfloat16 [32768, 2048], P('ctx', 'exp'), may hold values from -6 to 6
- memory_lookup_vectors: bfloat16 [64, 512, 2048], P(None, 'ctx', 'exp'), may hold values from -6 to 6
- content_vectors: bfloat16 [64, 512, 2048], P(None, 'ctx', 'exp'), may hold values from -6 to 6
- logit_multiplier: float32 [16], P('exp'), may hold values from 1 to 4
- chosen_tile_lists: int32 [64, 4], replicated, may hold values from 0 to 63, all different within a row
- premix_rmsnorm_scaling: float32 [2048], P('exp'), may hold values from 0.1 to 1.9
- routing_choice_ids: int32 [32768, 2], P('ctx'), may hold values from 0 to 63, all different within a row; in each aligned block of 256 rows (0 to 255, 256 to 511, ...) at most 12 rows name the same one
- routing_shares: float32 [32768, 2], P('ctx'), may hold values from 0.25 to 1
- gating_matrix: bfloat16 [128, 704, 2048], P('ctx', 'exp'), may hold values from -0.125 to 0.125
- raising_matrix: bfloat16 [128, 704, 2048], P('ctx', 'exp'), may hold values from -0.125 to 0.125
- lowering_matrix: bfloat16 [128, 704, 2048], P('ctx', None, 'exp'), may hold values from -0.15625 to 0.15625
Outputs:
- attended: bfloat16 [32768, 2048], P('ctx', 'exp')
- mixed: bfloat16 [32768, 2048], P('ctx', 'exp')
The draws below stay inside these ranges and needn't reach their ends.
Inputs may be any that keep to these rules, and one draw needn't show every extreme that they name: `chosen_tile_lists`: each row names 4 different blocks. `routing_choice_ids`: each event names 2 different experts; among the 256 events of one index of ctx (aligned blocks) at most 12 name one expert.
All inputs are finite; a program needn't handle non-finite values.
Results may differ from the reference program's by a relative error of at most 0.011.
Values may be sent and summed in bfloat16 or wider, within the bound.
A program may use at most 64 MiB of HBM per device.

```python
import math
import jax
import jax.numpy as jnp
import numpy as np
from jax import lax

D = 2048
ATTENTION_TOTAL = 16
FF = 1408
EXPERTS = 64
BLOCK = 512
TOPB = 4
TOK_DEV = 256
TOKENS = 32768
BLOCKS = 64
PER_HEAD_DIM = 128
SPLIT = 2
PIECES = 128
FFP = 704
CAP = 12
N_CTX = 128


def block_scale(stream_key, extent, shards, smallest, largest):
    loudness = 1.0
    for dim, blocks in shards:
        draws = jax.random.uniform(jax.random.fold_in(jax.random.fold_in(stream_key, 6), dim), (blocks,), jnp.float32, smallest / len(shards), largest / len(shards))
        loudness = loudness * jnp.repeat(jnp.exp(draws), extent[dim] // blocks).reshape((-1,) + (1,) * (len(extent) - 1 - dim))
    return loudness


def picks_of(rng, rows, amount, top, lift):
    sequence = jax.random.permutation(jax.random.fold_in(rng, 1), amount)
    pull = sequence
    for power in range(3):
        pull = pull * pull // amount
    pull = pull * lift // amount
    tickets = jax.random.randint(jax.random.fold_in(rng, 2), (rows, amount), 0, 4096) + pull
    sure = jax.random.permutation(jax.random.fold_in(rng, 3), rows)[jnp.arange(amount) % rows]
    tickets = jnp.where(jnp.arange(rows)[:, None] == sure[None, :], 1 << 14, tickets)
    merit = tickets * amount + jnp.arange(amount)
    return lax.top_k(merit.astype(jnp.int32), top)[1].astype(jnp.int32)


def routed_block(stream_key, own, number, rows, number_of, top, reach, slope):
    sequence = jax.random.permutation(stream_key, number_of)
    packed, usual = portions_of(number_of, rows * top, reach, slope, True), portions_of(number_of, rows * top, reach, slope, False)
    places = jnp.arange(number_of)

    def named(sizes, turn):
        used = int((sizes > 0).sum())
        fixed = max(1, used // 4)
        moved = fixed + (places - fixed + turn * (used - fixed)) % max(1, number_of - fixed)
        return jnp.zeros((number_of,), jnp.int32).at[sequence[jnp.where(places < fixed, places, moved)]].set(jnp.asarray(sizes, jnp.int32))

    sizes = jnp.where(number % 4 == 0, named(packed, number // 4), named(usual, number - number // 4 - 1))
    mixed = jax.random.permutation(jax.random.fold_in(own, 3), number_of)
    source_of, receiver = mixed[0:number_of // 2 * 2:2], mixed[1:number_of // 2 * 2:2]
    slack = jnp.minimum(sizes[source_of] - 1, reach - sizes[receiver]) // 2
    slack = jnp.where((source_of == sequence[0]) | (receiver == sequence[0]) | (sizes[receiver] == 0), 0, jnp.maximum(slack, 0))
    moved = jax.random.randint(jax.random.fold_in(own, 4), (number_of // 2,), 0, 1 << 20) % (slack + 1)
    sizes = sizes.at[source_of].add(-moved).at[receiver].add(moved)
    labels = jnp.searchsorted(jnp.cumsum(sizes), jnp.arange(rows * top), side="right").astype(jnp.int32)
    grid = labels.reshape(top, rows).T
    grid = grid[jax.random.permutation(jax.random.fold_in(own, 1), rows)]
    turn = jax.random.randint(jax.random.fold_in(own, 2), (rows, 1), 0, top)
    return jnp.take_along_axis(grid, (jnp.arange(top)[None, :] + turn) % top, axis=1)


def portions_of(number_of, total, reach, slope, full):
    loads = [(1 << 20) // math.isqrt(standing ** slope) + 1 for standing in range(1, number_of + 1)]
    largest = reach if full else min(reach, max(-(-total // number_of), total * loads[0] // sum(loads)))
    least = 1 if total - largest >= number_of - 1 else 0
    holding, rest = [largest] + [least] * (number_of - 1), total - largest - least * (number_of - 1)
    while rest > 0:
        movable = [i for i in range(1, number_of) if holding[i] < largest] or [i for i in range(1, number_of) if holding[i] < reach]
        pool, left = sum([loads[i] for i in movable]), rest
        for i in movable:
            extra = min(reach - holding[i], max(1, left * loads[i] // pool), rest)
            holding[i] = holding[i] + extra
            rest = rest - extra
    return np.array(holding)


def gaussian(key, dims, scale, limit, split=(), kind=jnp.bfloat16):
    level = block_scale(key, dims, split, -0.22, 0.18) if split else 1.0
    result = jax.random.normal(key, dims, jnp.float32) * scale * level
    return jnp.minimum(jnp.maximum(result, -limit), limit).astype(kind)


def setup_inputs(seed: int = 0) -> dict:
    key_list = jax.random.split(jax.random.key(seed), 13)
    hidden_state_stream = gaussian(key_list[0], (TOKENS, D), 1.0, 6.0, ((0, 128), (1, 4)))
    question_vectors = gaussian(key_list[1], (TOKENS, D), 1.0, 6.0, ((0, 128), (1, 4)))
    memory_lookup_vectors = gaussian(key_list[2], (BLOCKS, BLOCK, D), 1.0, 6.0, ((1, 128), (2, 4)))
    content_vectors = gaussian(key_list[3], (BLOCKS, BLOCK, D), 1.0, 6.0, ((1, 128), (2, 4)))
    logit_multiplier = jnp.clip(jnp.exp(math.log(4.0) - 1.3862944 * jax.random.uniform(key_list[4], (ATTENTION_TOTAL,), jnp.float32) ** block_scale(key_list[4], (ATTENTION_TOTAL,), ((0, 4),), -0.2, 0.2)), 1.0, 4.0)
    chosen_tile_lists = picks_of(key_list[5], BLOCKS, BLOCKS, TOPB, 1024)
    premix_rmsnorm_scaling = jnp.clip(1.0 + 0.18 * jax.random.normal(key_list[6], (D,), jnp.float32), 0.1, 1.9)
    routing_choice_ids_keys = jax.random.split(jax.random.fold_in(key_list[7], 1), TOKENS // TOK_DEV)
    routing_choice_ids_turns = jax.random.permutation(jax.random.fold_in(key_list[7], 3), TOKENS // TOK_DEV)
    routing_choice_ids = jax.vmap(lambda own, number: routed_block(jax.random.fold_in(key_list[7], 2), own, number, TOK_DEV, EXPERTS, 2, CAP, 2))(routing_choice_ids_keys, routing_choice_ids_turns).reshape((TOKENS, 2))
    routing_shares = jnp.clip(0.25 + 0.75 * jax.random.uniform(key_list[8], (TOKENS, 2), jnp.float32) ** block_scale(key_list[8], (TOKENS, 2), ((0, 128),), -0.2, 0.2), 0.25, 1.0)
    gating_matrix = gaussian(key_list[9], (PIECES, FFP, D), D ** -0.5, 0.125, ((0, 128), (1, 4)))
    raising_matrix = gaussian(key_list[10], (PIECES, FFP, D), D ** -0.5, 0.125, ((0, 128), (1, 4)))
    lowering_matrix = gaussian(key_list[11], (PIECES, FFP, D), FF ** -0.5, 0.15625, ((0, 128), (2, 4)))
    return {"hidden_state_stream": hidden_state_stream, "question_vectors": question_vectors, "memory_lookup_vectors": memory_lookup_vectors, "content_vectors": content_vectors, "logit_multiplier": logit_multiplier, "chosen_tile_lists": chosen_tile_lists, "premix_rmsnorm_scaling": premix_rmsnorm_scaling, "routing_choice_ids": routing_choice_ids, "routing_shares": routing_shares, "gating_matrix": gating_matrix, "raising_matrix": raising_matrix, "lowering_matrix": lowering_matrix}


def unit_rows(tensor, width):
    shaped = tensor.astype(jnp.float32).reshape(tensor.shape[:-1] + (tensor.shape[-1] // width, width))
    scaled = shaped * lax.rsqrt(lax.optimization_barrier(jnp.mean(shaped * shaped, axis=-1, keepdims=True)) + 1e-06)
    return scaled.reshape(tensor.shape).astype(jnp.bfloat16)

def slot_ranks(route_ids, experts):
    onehot = (route_ids[:, :, None] == jnp.arange(experts, dtype=jnp.int32)[None, None, :]).astype(jnp.int32)
    counts = lax.optimization_barrier(jnp.sum(onehot, axis=1))
    before = jnp.cumsum(counts, axis=0) - counts
    return lax.optimization_barrier(jnp.sum(onehot * before[:, None, :], axis=2)).astype(jnp.int32)

def reference(hidden_state_stream, question_vectors, memory_lookup_vectors, content_vectors, logit_multiplier, chosen_tile_lists, premix_rmsnorm_scaling, routing_choice_ids, routing_shares, gating_matrix, raising_matrix, lowering_matrix):
    query_unit = unit_rows(question_vectors, PER_HEAD_DIM).reshape(BLOCKS, BLOCK, ATTENTION_TOTAL, PER_HEAD_DIM)
    key_unit = unit_rows(memory_lookup_vectors, PER_HEAD_DIM)
    multiplier_vector = logit_multiplier / math.sqrt(PER_HEAD_DIM)

    def one_block(inputs):
        query_block, chosen = inputs
        key_rows = key_unit[chosen].reshape(TOPB * BLOCK, ATTENTION_TOTAL, PER_HEAD_DIM).astype(jnp.float32)
        value_rows = content_vectors[chosen].reshape(TOPB * BLOCK, ATTENTION_TOTAL, PER_HEAD_DIM).astype(jnp.float32)
        scores = jnp.einsum('qhd,khd->hqk', query_block.astype(jnp.float32), key_rows)
        expo = jnp.exp(scores * multiplier_vector[:, None, None])
        totals = lax.optimization_barrier(jnp.sum(expo, axis=2))
        expo_low = expo.astype(jnp.bfloat16).astype(jnp.float32)
        weighted = jnp.einsum('hqk,khd->qhd', expo_low, value_rows)
        return (weighted / jnp.transpose(totals)[:, :, None]).astype(jnp.bfloat16)
    attended = lax.map(one_block, (query_unit, chosen_tile_lists)).reshape(TOKENS, D)
    summed = hidden_state_stream.astype(jnp.float32) + attended.astype(jnp.float32)
    squares = lax.optimization_barrier(jnp.sum(summed * summed, axis=1))
    normed = (summed * lax.rsqrt(squares / D + 1e-05)[:, None] * premix_rmsnorm_scaling[None, :]).astype(jnp.bfloat16)
    ids_dev = routing_choice_ids.reshape(N_CTX, TOK_DEV, 2)
    ranks = jax.vmap(lambda route_ids: slot_ranks(route_ids, EXPERTS))(ids_dev)
    source = jnp.arange(N_CTX, dtype=jnp.int32)[:, None, None]
    position = (source * CAP + ranks).reshape(-1).astype(jnp.int32)
    token_index = jnp.broadcast_to(jnp.arange(TOKENS, dtype=jnp.int32).reshape(N_CTX, TOK_DEV, 1), (N_CTX, TOK_DEV, 2)).reshape(-1)
    flat_ids = routing_choice_ids.reshape(-1).astype(jnp.int32)
    slot_token = jnp.full((EXPERTS, N_CTX * CAP), TOKENS, jnp.int32).at[flat_ids, position].set(token_index)
    slot_gate = jnp.zeros((EXPERTS, N_CTX * CAP), jnp.float32).at[flat_ids, position].set(routing_shares.reshape(-1))
    normed_pad = jnp.concatenate([normed, jnp.zeros((1, D), jnp.bfloat16)], axis=0)

    def piece_step(total, inputs):
        gate_piece, up_piece, down_piece, index = inputs
        expert = index // SPLIT
        rows_index = slot_token[expert]
        rows = normed_pad[rows_index]
        gate_out = jnp.dot(rows, gate_piece.T, preferred_element_type=jnp.float32)
        up_out = jnp.dot(rows, up_piece.T, preferred_element_type=jnp.float32)
        act = (jax.nn.silu(gate_out) * up_out).astype(jnp.bfloat16)
        piece_out = jnp.dot(act, down_piece, preferred_element_type=jnp.float32).astype(jnp.bfloat16)
        total = total.at[rows_index].add(slot_gate[expert][:, None] * piece_out.astype(jnp.float32))
        return (total, None)
    start = jnp.zeros((TOKENS + 1, D), jnp.float32)
    expert_sum, _ = lax.scan(piece_step, start, (gating_matrix, raising_matrix, lowering_matrix, jnp.arange(PIECES, dtype=jnp.int32)))
    mixed = (summed + expert_sum[:TOKENS]).astype(jnp.bfloat16)
    return (attended, mixed)
```

```python
import functools
import math

import jax
import jax.numpy as jnp
from jax import lax
from jax.experimental import pallas as pl
from jax.experimental.pallas import tpu as pltpu
from jax.sharding import PartitionSpec as P

D = 2048
EXPERTS = 64
CAP = 12
N = 128
GROUPS = 4
MESH = pl.DeviceIdType.MESH
F32 = jnp.float32
BF16 = jnp.bfloat16

NT = (((1,), (1,)), ((), ()))


def unit_heads(x):
    parts = []
    for h in range(x.shape[1] // 128):
        s = x[:, 128 * h : 128 * (h + 1)].astype(F32)
        parts.append(s * lax.rsqrt(jnp.mean(s * s, axis=1, keepdims=True) + 1e-06))
    return jnp.concatenate(parts, axis=1).astype(BF16)


def layer_kernel(
    mult_ref,
    hid_ref,
    q_ref,
    k_ref,
    v_ref,
    src_ref,
    gain_ref,
    ids_ref,
    share_ref,
    gate_ref,
    up_ref,
    down_ref,
    att_ref,
    mix_ref,
    kvs,
    kvr,
    qbuf,
    qsend,
    hbuf,
    gbuf,
    obuf,
    osend,
    acc,
    den,
    disp,
    comb_hi,
    comb_lo,
    rows32,
    dsend,
    drecv,
    xbuf,
    act,
    rsend,
    rrecv,
    ysend,
    yrecv,
    wg,
    wu,
    wd,
    sems,
    kv_sem,
):
    me = lax.axis_index("ctx")
    f = lax.axis_index("exp")
    i = lax.rem(me, 2)
    nb = me + 1 - 2 * i
    f1 = f + 1 - 2 * lax.rem(f, 2)
    f2 = lax.rem(f + 2, 4)
    f3 = 3 - f
    (KVS, QS, QR, HS, HR, GS, GR, OS, OR, DS, DR, RS, RR, YS, YR, WS, WX, WC, WF, WFS, WT, LOCW) = range(22)

    bar = pltpu.get_barrier_semaphore()

    def greet(k, carry):
        pl.semaphore_signal(bar, inc=1, device_id=(lax.rem(me + k, N), f), device_id_type=MESH)
        return carry

    lax.fori_loop(1, N, greet, 0)
    for g in (f1, f2, f3):
        pl.semaphore_signal(bar, inc=1, device_id=(me, g), device_id_type=MESH)
        pl.semaphore_signal(bar, inc=1, device_id=(nb, g), device_id_type=MESH)

    pick = (lax.broadcasted_iota(jnp.int32, (256, 1024), 0) == src_ref[...]).astype(F32)
    pick = jnp.transpose(pick).astype(BF16)
    kunit = unit_heads(k_ref[...])
    for half in range(2):
        cols = slice(256 * half, 256 * (half + 1))
        got = jnp.dot(pick, kunit[:, cols], preferred_element_type=F32).astype(BF16)
        kvs[:, half, 0:16, :] = got.reshape(64, 16, 256)
        got = jnp.dot(pick, v_ref[:, cols], preferred_element_type=F32).astype(BF16)
        kvs[:, half, 16:32, :] = got.reshape(64, 16, 256)
    qunit = unit_heads(q_ref[...])
    first = jnp.broadcast_to(i, (256, 256)) == 0
    qbuf[i] = jnp.where(first, qunit[:, :256], qunit[:, 256:])
    qsend[...] = jnp.where(first, qunit[:, 256:], qunit[:, :256])

    pl.semaphore_wait(bar, N - 1 + 6)

    def remote(src, dst, s, r, ctx, ex):
        return pltpu.make_async_remote_copy(
            src, dst, sems.at[s], r, device_id=(ctx, ex), device_id_type=MESH
        )

    def wait(ref, sem):
        pltpu.make_async_copy(ref, ref, sem).wait()

    remote(qsend, qbuf.at[i], QS, sems.at[QR], nb, f).start()
    own_kv = pltpu.make_async_copy(kvs.at[me // 2, i], kvr.at[0], kv_sem.at[0])
    own_kv.start()

    def send_kv(k, carry):
        d = lax.rem(me + k, N)
        remote(
            kvs.at[d // 2, lax.rem(d, 2)], kvr.at[k], KVS, kv_sem.at[k // (N // GROUPS)], d, f
        ).start()
        return carry

    lax.fori_loop(1, N // GROUPS, send_kv, 0)

    own_rows = pl.ds(pl.multiple_of(f * 176, 16), 176)
    for g, left, sem in ((f2, WS, WX), (f1, WT, WC)):
        remote(gate_ref.at[0], wg.at[own_rows], left, sems.at[sem], me, g).start()
        remote(up_ref.at[0], wu.at[own_rows], left, sems.at[sem], me, g).start()
        remote(down_ref.at[0], wd.at[f], left, sems.at[sem], me, g).start()
    local_w = [
        pltpu.make_async_copy(gate_ref.at[0], wg.at[own_rows], sems.at[LOCW]),
        pltpu.make_async_copy(up_ref.at[0], wu.at[own_rows], sems.at[LOCW]),
        pltpu.make_async_copy(down_ref.at[0], wd.at[f], sems.at[LOCW]),
    ]
    for c in local_w:
        c.start()
    lax.fori_loop(N // GROUPS, N, send_kv, 0)

    for g in (f1, f2, f3):
        remote(hid_ref, hbuf.at[f], HS, sems.at[HR], me, g).start()
        remote(gain_ref, gbuf.at[f], GS, sems.at[GR], me, g).start()
    hbuf[f] = hid_ref[...]
    gbuf[f] = gain_ref[...]

    ids = ids_ref[...]
    experts = lax.broadcasted_iota(jnp.int32, (EXPERTS, 256), 0)
    named = [(experts == ids[c : c + 1, :]).astype(F32) for c in range(2)]
    counts = (named[0] + named[1]).astype(BF16)
    earlier = (
        lax.broadcasted_iota(jnp.int32, (256, 256), 0) < lax.broadcasted_iota(jnp.int32, (256, 256), 1)
    ).astype(F32).astype(BF16)
    before = jnp.dot(counts, earlier, preferred_element_type=F32)
    keys = []
    for c in range(2):
        rank = jnp.sum(named[c] * before, axis=0, keepdims=True)
        keys.append(ids[c : c + 1, :] * CAP + rank.astype(jnp.int32))
    row = lax.broadcasted_iota(jnp.int32, (192, 256), 0)
    expert = (row * 171) // 512
    slot = expert * CAP + (row - expert * 3)
    mine = slot + 3 * f
    disp[...] = ((keys[0] == mine) | (keys[1] == mine)).astype(F32).astype(BF16)
    for g in range(4):
        there = slot + 3 * g
        table = jnp.where(keys[0] == there, share_ref[0:1, :], 0.0) + jnp.where(
            keys[1] == there, share_ref[1:2, :], 0.0
        )
        high = table.astype(BF16).astype(F32)
        comb_hi[g] = jnp.transpose(high).astype(BF16)
        comb_lo[g] = jnp.transpose(table - high).astype(BF16)

    acc[...] = jnp.zeros_like(acc)
    den[...] = jnp.zeros_like(den)
    wait(qbuf.at[0], sems.at[QR])
    per = N // GROUPS

    def attend(grp, carry):
        wait(kvr.at[pl.ds(0, per)], kv_sem.at[grp])
        span = pl.ds(pl.multiple_of(grp * per, per), per)
        kg = kvr[span, 0:16, :].reshape(per * 16, 256)
        vg = kvr[span, 16:32, :].reshape(per * 16, 256)
        for h in range(2):
            cols = slice(128 * h, 128 * (h + 1))
            scale = mult_ref[2 * i + h] * (1.0 / math.sqrt(128.0))
            for j in range(2):
                s = lax.dot_general(qbuf[j, :, cols], kg[:, cols], NT, preferred_element_type=F32)
                e = jnp.exp(s * scale)
                total = e[:, 0:128]
                for c in range(1, per * 16 // 128):
                    total = total + e[:, 128 * c : 128 * (c + 1)]
                den[j, h] += total
                acc[j, h] += jnp.dot(e.astype(BF16), vg[:, cols], preferred_element_type=F32)
        return carry

    lax.fori_loop(0, GROUPS, attend, 0)
    for j in range(2):
        for h in range(2):
            out = acc[j, h] / jnp.sum(den[j, h], axis=1, keepdims=True)
            osend[j, :, 128 * h : 128 * (h + 1)] = out.astype(BF16)

    mark = 2 * f + i
    for g in (f1, f2, f3):
        remote(osend.at[i], obuf.at[mark], OS, sems.at[OR], me, g).start()
    for g in (f, f1, f2, f3):
        remote(osend.at[1 - i], obuf.at[mark], OS, sems.at[OR], nb, g).start()
    obuf[mark] = osend[i]
    wait(hbuf.at[pl.ds(0, 3)], sems.at[HR])
    wait(gbuf.at[pl.ds(0, 3)], sems.at[GR])
    wait(obuf.at[pl.ds(0, 7)], sems.at[OR])

    squares = jnp.zeros((256, 1), F32)
    for s in range(8):
        cols = slice(256 * (s % 2), 256 * (s % 2) + 256)
        part = hbuf[s // 2, :, cols].astype(F32) + obuf[s].astype(F32)
        squares = squares + jnp.sum(part * part, axis=1, keepdims=True)
    inverse = lax.rsqrt(squares / D + 1e-05)
    for s in range(8):
        cols = slice(256 * (s % 2), 256 * (s % 2) + 256)
        part = hbuf[s // 2, :, cols].astype(F32) + obuf[s].astype(F32)
        unit = (part * inverse * gbuf[s // 2, 0:1, cols]).astype(BF16)
        sent = jnp.dot(disp[...], unit, preferred_element_type=F32)
        for c in range(2):
            rows32[pl.ds(2 * s + c, 192, stride=16), :] = sent[:, 128 * c : 128 * (c + 1)]
    for b in range(8):
        dsend[pl.ds(8 * b, 8)] = rows32[pl.ds(384 * b, 384), :].astype(BF16).reshape(8, 48, 128)

    own_d = pltpu.make_async_copy(dsend.at[me // 2], drecv.at[0], sems.at[DR])
    own_d.start()

    def send_rows(k, carry):
        d = lax.rem(me + k, N)
        remote(dsend.at[d // 2], drecv.at[k], DS, sems.at[DR], d, f).start()
        return carry

    lax.fori_loop(1, N, send_rows, 0)

    three = pl.ds(0, 528)
    wait(wg.at[three], sems.at[WX])
    rows2 = pl.ds(pl.multiple_of(f2 * 176, 16), 176)
    remote(wg.at[rows2], wg.at[rows2], WFS, sems.at[WF], me, f1).start()
    remote(wu.at[rows2], wu.at[rows2], WFS, sems.at[WF], me, f1).start()
    remote(wd.at[f2], wd.at[f2], WFS, sems.at[WF], me, f1).start()
    wait(wg.at[three], sems.at[LOCW])
    wait(wg.at[three], sems.at[WC])
    wait(wg.at[three], sems.at[WF])

    wait(drecv, sems.at[DR])

    def widen(b, carry):
        rows32[pl.ds(pl.multiple_of(384 * b, 384), 384), :] = (
            drecv[pl.ds(pl.multiple_of(8 * b, 8), 8)].reshape(384, 128).astype(F32)
        )
        return carry

    lax.fori_loop(0, 16, widen, 0)
    for c in range(16):
        xbuf[:, 128 * c : 128 * (c + 1)] = rows32[pl.ds(c, 384, stride=16), :].astype(BF16)
    for lo, hi in ((0, 256), (256, 512), (512, 704)):
        gate = lax.dot_general(xbuf[...], wg[lo:hi, :], NT, preferred_element_type=F32)
        up = lax.dot_general(xbuf[...], wu[lo:hi, :], NT, preferred_element_type=F32)
        act[:, lo:hi] = (gate / (1.0 + jnp.exp(-gate)) * up).astype(BF16)
    for g in range(4):
        out = jnp.dot(act[...], wd[g], preferred_element_type=F32)
        for c in range(4):
            rows32[pl.ds(4 * g + c, 384, stride=16), :] = out[:, 128 * c : 128 * (c + 1)]

    def narrow(b, carry):
        rsend[pl.ds(pl.multiple_of(8 * b, 8), 8)] = (
            rows32[pl.ds(pl.multiple_of(384 * b, 384), 384), :].astype(BF16).reshape(8, 48, 128)
        )
        return carry

    lax.fori_loop(0, 16, narrow, 0)
    own_r = pltpu.make_async_copy(rsend.at[0], rrecv.at[me], sems.at[RR])
    own_r.start()

    def send_back(k, carry):
        d = lax.rem(me + N - k, N)
        remote(rsend.at[k], rrecv.at[me], RS, sems.at[RR], d, f).start()
        return carry

    lax.fori_loop(1, N, send_back, 0)
    wait(rrecv, sems.at[RR])

    def pieces(b, carry):
        pair = rrecv[pl.ds(pl.multiple_of(16 * b, 16), 16)].astype(F32).reshape(8, 2, 48, 128)
        rows32[pl.ds(pl.multiple_of(384 * b, 384), 384), :] = (pair[:, 0] + pair[:, 1]).reshape(384, 128)
        return carry

    lax.fori_loop(0, 8, pieces, 0)
    for c in range(16):
        ysend[c // 4, :, 128 * (c % 4) : 128 * (c % 4) + 128] = rows32[
            pl.ds(c, 192, stride=16), :
        ].astype(BF16)
    for g in (f2, f3, f1):
        remote(ysend.at[g], yrecv.at[f], YS, sems.at[YR], me, g).start()
    yrecv[f] = ysend[f]
    wait(yrecv.at[pl.ds(0, 3)], sems.at[YR])

    total = jnp.zeros((256, 512), F32)
    for g in range(4):
        total = total + jnp.dot(comb_hi[g], yrecv[g], preferred_element_type=F32)
        total = total + jnp.dot(comb_lo[g], yrecv[g], preferred_element_type=F32)
    for s in range(2):
        cols = slice(256 * s, 256 * (s + 1))
        mine_o = obuf[2 * f + s]
        att_ref[:, cols] = mine_o
        summed = hid_ref[:, cols].astype(F32) + mine_o.astype(F32)
        mix_ref[:, cols] = (summed + total[:, cols]).astype(BF16)

    wait(qsend, sems.at[QS])
    wait(kvr.at[pl.ds(0, N - 1)], sems.at[KVS])
    wait(hbuf.at[pl.ds(0, 3)], sems.at[HS])
    wait(gbuf.at[pl.ds(0, 3)], sems.at[GS])
    wait(obuf.at[pl.ds(0, 7)], sems.at[OS])
    wait(drecv.at[pl.ds(0, N - 1)], sems.at[DS])
    wait(rrecv.at[pl.ds(0, N - 1)], sems.at[RS])
    wait(yrecv.at[pl.ds(0, 3)], sems.at[YS])
    wait(wg.at[three], sems.at[WFS])
    wait(wg.at[three], sems.at[WS])
    wait(wg.at[three], sems.at[WT])


def per_device(
    hidden_state_stream,
    question_vectors,
    memory_lookup_vectors,
    content_vectors,
    logit_multiplier,
    chosen_tile_lists,
    premix_rmsnorm_scaling,
    routing_choice_ids,
    routing_shares,
    gating_matrix,
    raising_matrix,
    lowering_matrix,
):
    src = (chosen_tile_lists[:, :, None] * 4 + jnp.arange(4, dtype=jnp.int32)).reshape(1, 1024)
    gain = jnp.broadcast_to(premix_rmsnorm_scaling[None, :], (8, 512))
    vmem = pl.BlockSpec(memory_space=pltpu.VMEM)
    hbm = pl.BlockSpec(memory_space=pl.ANY)
    scratch = [
        pltpu.VMEM((64, 2, 32, 256), BF16),
        pltpu.VMEM((N, 32, 256), BF16),
        pltpu.VMEM((2, 256, 256), BF16),
        pltpu.VMEM((256, 256), BF16),
        pltpu.VMEM((4, 256, 512), BF16),
        pltpu.VMEM((4, 8, 512), F32),
        pltpu.VMEM((8, 256, 256), BF16),
        pltpu.VMEM((2, 256, 256), BF16),
        pltpu.VMEM((2, 2, 256, 128), F32),
        pltpu.VMEM((2, 2, 256, 128), F32),
        pltpu.VMEM((192, 256), BF16),
        pltpu.VMEM((4, 256, 192), BF16),
        pltpu.VMEM((4, 256, 192), BF16),
        pltpu.VMEM((6144, 128), F32),
        pltpu.VMEM((64, 48, 128), BF16),
        pltpu.VMEM((N, 48, 128), BF16),
        pltpu.VMEM((384, 2048), BF16),
        pltpu.VMEM((384, 704), BF16),
        pltpu.VMEM((N, 48, 128), BF16),
        pltpu.VMEM((N, 48, 128), BF16),
        pltpu.VMEM((4, 192, 512), BF16),
        pltpu.VMEM((4, 192, 512), BF16),
        pltpu.VMEM((704, 2048), BF16),
        pltpu.VMEM((704, 2048), BF16),
        pltpu.VMEM((4, 704, 512), BF16),
        pltpu.SemaphoreType.DMA((22,)),
        pltpu.SemaphoreType.DMA((GROUPS,)),
    ]
    shape = jax.ShapeDtypeStruct((256, 512), BF16)
    return pl.pallas_call(
        layer_kernel,
        out_shape=(shape, shape),
        in_specs=[pl.BlockSpec(memory_space=pltpu.SMEM)] + [vmem] * 8 + [hbm] * 3,
        out_specs=(vmem, vmem),
        scratch_shapes=scratch,
        name="layer",
        cost_estimate=pl.CostEstimate(flops=5_000_000_000, bytes_accessed=20_000_000, transcendentals=3_000_000),
        compiler_params=pltpu.CompilerParams(
            collective_id=1, has_side_effects=True, vmem_limit_bytes=52 * 2**20
        ),
    )(
        logit_multiplier,
        hidden_state_stream,
        question_vectors,
        memory_lookup_vectors.reshape(256, 512),
        content_vectors.reshape(256, 512),
        src,
        gain,
        routing_choice_ids.T,
        routing_shares.T,
        gating_matrix,
        raising_matrix,
        lowering_matrix,
    )


def solution(mesh):
    in_specs = (
        P("ctx", "exp"),
        P("ctx", "exp"),
        P(None, "ctx", "exp"),
        P(None, "ctx", "exp"),
        P("exp"),
        P(),
        P("exp"),
        P("ctx", None),
        P("ctx", None),
        P("ctx", "exp", None),
        P("ctx", "exp", None),
        P("ctx", None, "exp"),
    )
    out_specs = (P("ctx", "exp"), P("ctx", "exp"))
    return jax.shard_map(
        per_device, mesh=mesh, in_specs=in_specs, out_specs=out_specs, check_vma=False
    )
```

```python
import functools
import math

import jax
import jax.numpy as jnp
from jax import lax
from jax.experimental import pallas as pl
from jax.experimental.pallas import tpu as pltpu
from jax.sharding import PartitionSpec as P

D = 2048
EXPERTS = 64
CAP = 12
N = 128
GROUPS = 4
MESH = pl.DeviceIdType.MESH
F32 = jnp.float32
BF16 = jnp.bfloat16

NT = (((1,), (1,)), ((), ()))


def unit_heads(x):
    parts = []
    for h in range(x.shape[1] // 128):
        s = x[:, 128 * h : 128 * (h + 1)].astype(F32)
        parts.append(s * lax.rsqrt(jnp.mean(s * s, axis=1, keepdims=True) + 1e-06))
    return jnp.concatenate(parts, axis=1).astype(BF16)


def layer_kernel(
    mult_ref,
    hid_ref,
    q_ref,
    k_ref,
    v_ref,
    src_ref,
    gain_ref,
    ids_ref,
    share_ref,
    gate_ref,
    up_ref,
    down_ref,
    att_ref,
    mix_ref,
    kvs,
    kvr,
    qbuf,
    qsend,
    hbuf,
    gbuf,
    obuf,
    osend,
    acc,
    den,
    disp,
    comb_hi,
    comb_lo,
    rows32,
    dsend,
    drecv,
    xbuf,
    abuf,
    psend,
    precv,
    rsend,
    rrecv,
    ybuf,
    wg,
    wu,
    wd,
    sems,
    kv_sem,
    d_sem,
    fwd_sem,
    p_sem,
    a_sem,
):
    me = lax.axis_index("ctx")
    f = lax.axis_index("exp")
    i = lax.rem(me, 2)
    nb = me + 1 - 2 * i
    f1 = f + 1 - 2 * lax.rem(f, 2)
    f2 = lax.rem(f + 2, 4)
    f3 = 3 - f
    mz = lax.rem(me, 8)
    my = lax.rem(me // 8, 8)
    mx = me // 64
    zp = mz // 2
    (KVS, QS, QR, HS, HX, HC, HF, HFS, GS, GR, OS, OR, DS, FS, PS, RS, RR) = range(17)
    (WS, WX, WT, WC, WF, WFS, US, UX, UT, UC, UF, UFS, LOCW) = range(17, 30)

    bar = pltpu.get_barrier_semaphore()

    def greet(k, carry):
        pl.semaphore_signal(bar, inc=1, device_id=(lax.rem(me + k, N), f), device_id_type=MESH)
        return carry

    lax.fori_loop(1, N, greet, 0)
    for g in (f1, f2, f3):
        pl.semaphore_signal(bar, inc=1, device_id=(me, g), device_id_type=MESH)
        pl.semaphore_signal(bar, inc=1, device_id=(nb, g), device_id_type=MESH)

    pick = (lax.broadcasted_iota(jnp.int32, (256, 1024), 0) == src_ref[...]).astype(F32)
    pick = jnp.transpose(pick).astype(BF16)
    kunit = unit_heads(k_ref[...])
    for half in range(2):
        cols = slice(256 * half, 256 * (half + 1))
        got = jnp.dot(pick, kunit[:, cols], preferred_element_type=F32).astype(BF16)
        kvs[:, half, 0:16, :] = got.reshape(64, 16, 256)
        got = jnp.dot(pick, v_ref[:, cols], preferred_element_type=F32).astype(BF16)
        kvs[:, half, 16:32, :] = got.reshape(64, 16, 256)

    pl.semaphore_wait(bar, N - 1 + 6)

    def remote(src, dst, s, r, ctx, ex):
        return pltpu.make_async_remote_copy(
            src, dst, sems.at[s], r, device_id=(ctx, ex), device_id_type=MESH
        )

    def wait(ref, sem):
        pltpu.make_async_copy(ref, ref, sem).wait()

    own_kv = pltpu.make_async_copy(kvs.at[me // 2, i], kvr.at[0], kv_sem.at[0])
    own_kv.start()

    def send_kv(k, carry):
        d = lax.rem(me + k, N)
        remote(
            kvs.at[d // 2, lax.rem(d, 2)], kvr.at[k], KVS, kv_sem.at[k // (N // GROUPS)], d, f
        ).start()
        return carry

    lax.fori_loop(1, N // GROUPS, send_kv, 0)

    def shard(who, lo, hi):
        return pl.ds(pl.multiple_of(who * 176 + lo, 16), hi - lo)

    for g, left, sem in ((f2, WS, WX), (f1, WT, WC)):
        remote(gate_ref.at[0], wg.at[shard(f, 0, 176)], left, sems.at[sem], me, g).start()
        remote(up_ref.at[0, 0:96], wu.at[shard(f, 0, 96)], left, sems.at[sem], me, g).start()
    for c in (
        pltpu.make_async_copy(gate_ref.at[0], wg.at[shard(f, 0, 176)], sems.at[LOCW]),
        pltpu.make_async_copy(up_ref.at[0], wu.at[shard(f, 0, 176)], sems.at[LOCW]),
        pltpu.make_async_copy(down_ref.at[0], wd, sems.at[LOCW]),
    ):
        c.start()
    lax.fori_loop(N // GROUPS, N, send_kv, 0)

    qunit = unit_heads(q_ref[...])
    first = jnp.broadcast_to(i, (256, 256)) == 0
    qbuf[i] = jnp.where(first, qunit[:, :256], qunit[:, 256:])
    qsend[...] = jnp.where(first, qunit[:, 256:], qunit[:, :256])
    remote(qsend, qbuf.at[i], QS, sems.at[QR], nb, f).start()

    for g, sem in ((f2, HX), (f1, HC)):
        remote(hid_ref, hbuf.at[f], HS, sems.at[sem], me, g).start()
    for g in (f1, f2, f3):
        remote(gain_ref, gbuf.at[f], GS, sems.at[GR], me, g).start()
    hbuf[f] = hid_ref[...]
    gbuf[f] = gain_ref[...]

    ids = ids_ref[...]
    experts = lax.broadcasted_iota(jnp.int32, (EXPERTS, 256), 0)
    named = [(experts == ids[c : c + 1, :]).astype(F32) for c in range(2)]
    counts = (named[0] + named[1]).astype(BF16)
    earlier = (
        lax.broadcasted_iota(jnp.int32, (256, 256), 0) < lax.broadcasted_iota(jnp.int32, (256, 256), 1)
    ).astype(F32).astype(BF16)
    before = jnp.dot(counts, earlier, preferred_element_type=F32)
    keys = []
    for c in range(2):
        rank = jnp.sum(named[c] * before, axis=0, keepdims=True)
        keys.append(ids[c : c + 1, :] * CAP + rank.astype(jnp.int32))
    row = lax.broadcasted_iota(jnp.int32, (192, 256), 0)
    expert = (row * 171) // 512
    slot = expert * CAP + (row - expert * 3)
    mine = slot + 3 * f
    disp[...] = ((keys[0] == mine) | (keys[1] == mine)).astype(F32).astype(BF16)
    for b in range(3):
        line = lax.broadcasted_iota(jnp.int32, (256, 256), 0) + 256 * b
        expert = (line * 5462) // 65536
        inner = line - expert * 12
        there = expert * CAP + 3 * lax.rem(inner, 4) + inner // 4
        table = jnp.where(keys[0] == there, share_ref[0:1, :], 0.0) + jnp.where(
            keys[1] == there, share_ref[1:2, :], 0.0
        )
        high = table.astype(BF16).astype(F32)
        comb_hi[:, 256 * b : 256 * (b + 1)] = jnp.transpose(high).astype(BF16)
        comb_lo[:, 256 * b : 256 * (b + 1)] = jnp.transpose(table - high).astype(BF16)

    acc[...] = jnp.zeros_like(acc)
    den[...] = jnp.zeros_like(den)
    wait(qbuf.at[0], sems.at[QR])
    per = N // GROUPS

    def attend(grp, carry):
        wait(kvr.at[pl.ds(0, per)], kv_sem.at[grp])
        span = pl.ds(pl.multiple_of(grp * per, per), per)
        kg = kvr[span, 0:16, :].reshape(per * 16, 256)
        vg = kvr[span, 16:32, :].reshape(per * 16, 256)
        for h in range(2):
            cols = slice(128 * h, 128 * (h + 1))
            scale = mult_ref[2 * i + h] * (1.0 / math.sqrt(128.0))
            for j in range(2):
                s = lax.dot_general(qbuf[j, :, cols], kg[:, cols], NT, preferred_element_type=F32)
                e = jnp.exp(s * scale)
                total = e[:, 0:128]
                for c in range(1, per * 16 // 128):
                    total = total + e[:, 128 * c : 128 * (c + 1)]
                den[j, h] += total
                acc[j, h] += jnp.dot(e.astype(BF16), vg[:, cols], preferred_element_type=F32)
        return carry

    lax.fori_loop(0, GROUPS, attend, 0)
    for j in range(2):
        for h in range(2):
            out = acc[j, h] / jnp.sum(den[j, h], axis=1, keepdims=True)
            osend[j, :, 128 * h : 128 * (h + 1)] = out.astype(BF16)

    wait(hbuf.at[0], sems.at[HX])
    remote(hbuf.at[f2], hbuf.at[f2], HFS, sems.at[HF], me, f1).start()
    mark = 2 * f + i
    for g in (f1, f2, f3):
        remote(osend.at[i], obuf.at[mark], OS, sems.at[OR], me, g).start()
    for g in (f, f1, f2, f3):
        remote(osend.at[1 - i], obuf.at[mark], OS, sems.at[OR], nb, g).start()
    obuf[mark] = osend[i]
    early = pl.ds(0, 272)
    wait(wg.at[early], sems.at[WX])
    remote(wg.at[shard(f2, 0, 176)], wg.at[shard(f2, 0, 176)], WFS, sems.at[WF], me, f1).start()
    remote(wu.at[shard(f2, 0, 96)], wu.at[shard(f2, 0, 96)], WFS, sems.at[WF], me, f1).start()
    wait(hbuf.at[0], sems.at[HC])
    wait(hbuf.at[0], sems.at[HF])
    wait(gbuf.at[pl.ds(0, 3)], sems.at[GR])
    wait(obuf.at[pl.ds(0, 7)], sems.at[OR])

    squares = jnp.zeros((256, 1), F32)
    for s in range(8):
        cols = slice(256 * (s % 2), 256 * (s % 2) + 256)
        part = hbuf[s // 2, :, cols].astype(F32) + obuf[s].astype(F32)
        squares = squares + jnp.sum(part * part, axis=1, keepdims=True)
    inverse = lax.rsqrt(squares / D + 1e-05)
    for s in range(8):
        cols = slice(256 * (s % 2), 256 * (s % 2) + 256)
        part = hbuf[s // 2, :, cols].astype(F32) + obuf[s].astype(F32)
        unit = (part * inverse * gbuf[s // 2, 0:1, cols]).astype(BF16)
        sent = jnp.dot(disp[...], unit, preferred_element_type=F32)
        for c in range(2):
            rows32[pl.ds(2 * s + c, 192, stride=16), :] = sent[:, 128 * c : 128 * (c + 1)]
    for b in range(8):
        dsend[pl.ds(8 * b, 8)] = rows32[pl.ds(384 * b, 384), :].astype(BF16).reshape(8, 48, 128)

    def near(q, sign):
        x = lax.rem(mx + 2 + sign * lax.rem(q, 2), 2)
        y = lax.rem(my + 8 + sign * (q // 2), 8)
        return x * 64 + y * 8

    def send_rows(q, kinds):
        column = near(q, 1)
        for off, member, slot_ in (
            (0, i, 0),
            (1, 0, 1 + i),
            (3, 1, 1 + i),
            (2, 1 - i, 3),
        )[kinds]:
            pair = lax.rem(zp + off, 4)
            remote(
                dsend.at[column // 2 + pair],
                drecv.at[1, 4 * q + slot_],
                DS,
                d_sem.at[q // 4],
                column + 2 * pair + member,
                f,
            ).start()

    own_d = pltpu.make_async_copy(dsend.at[me // 2], drecv.at[1, 0], d_sem.at[0])
    own_d.start()
    send_rows(0, slice(1, 4))

    def send_column(q, carry):
        send_rows(q, slice(0, 4))
        return carry

    lax.fori_loop(1, 16, send_column, 0)

    for g, left, sem in ((f2, US, UX), (f1, UT, UC)):
        remote(up_ref.at[0, 96:176], wu.at[shard(f, 96, 176)], left, sems.at[sem], me, g).start()

    def pass_on(g, carry):
        span = pl.ds(pl.multiple_of(16 * g, 16), 16)
        wait(drecv.at[1, pl.ds(0, 16)], d_sem.at[g])
        remote(drecv.at[1, span], drecv.at[0, span], FS, fwd_sem.at[g], nb, f).start()
        return carry

    lax.fori_loop(0, 4, pass_on, 0)

    late = pl.ds(0, 80)
    wait(wg.at[late], sems.at[UX])
    remote(wu.at[shard(f2, 96, 176)], wu.at[shard(f2, 96, 176)], UFS, sems.at[UF], me, f1).start()
    wait(wg.at[pl.ds(0, 528)], sems.at[LOCW])
    wait(wg.at[early], sems.at[WC])
    wait(wg.at[early], sems.at[WF])
    wait(wg.at[late], sems.at[UC])
    wait(wg.at[late], sems.at[UF])

    def hidden(half):
        def widen(b, carry):
            rows32[pl.ds(pl.multiple_of(384 * b, 384), 384), :] = (
                drecv[half, pl.ds(pl.multiple_of(8 * b, 8), 8)].reshape(384, 128).astype(F32)
            )
            return carry

        lax.fori_loop(0, 8, widen, 0)
        for c in range(16):
            xbuf[:, 128 * c : 128 * (c + 1)] = rows32[pl.ds(c, 192, stride=16), :].astype(BF16)
        for lo, hi in ((0, 256), (256, 512), (512, 704)):
            gate = lax.dot_general(xbuf[...], wg[lo:hi, :], NT, preferred_element_type=F32)
            up = lax.dot_general(xbuf[...], wu[lo:hi, :], NT, preferred_element_type=F32)
            abuf[half, f, :, lo:hi] = (gate / (1.0 + jnp.exp(-gate)) * up).astype(BF16)
        here = abuf.at[half, f]
        remote(here, here, 6 * half + 30, a_sem.at[half, 0], me, f2).start()
        remote(here, here, 6 * half + 31, a_sem.at[half, 1], me, f1).start()

    def share_on(half):
        there = abuf.at[half, f2]
        wait(there, a_sem.at[half, 0])
        remote(there, there, 6 * half + 32, a_sem.at[half, 2], me, f1).start()

    def lower(half):
        for s in (1, 2):
            wait(abuf.at[half, 0], a_sem.at[half, s])
        for g in range(4):
            out = jnp.dot(abuf[half, g], wd[...], preferred_element_type=F32)
            for c in range(4):
                rows32[pl.ds(4 * g + c, 192, stride=16), :] = out[:, 128 * c : 128 * (c + 1)]

    hidden(1)
    share_on(1)
    for g in range(4):
        wait(drecv.at[0, pl.ds(0, 16)], fwd_sem.at[g])
    hidden(0)
    share_on(0)
    lower(0)

    def partner(g, carry):
        span = pl.ds(pl.multiple_of(16 * g, 16), 16)
        psend[span] = (
            rows32[pl.ds(pl.multiple_of(768 * g, 768), 768), :].astype(BF16).reshape(16, 48, 128)
        )
        remote(psend.at[span], precv.at[span], PS, p_sem.at[g], nb, f).start()
        return carry

    lax.fori_loop(0, 4, partner, 0)
    lower(1)

    def send_back(q, kinds):
        column = near(q, -1)
        side = 2 * lax.rem(zp + 3 + 2 * i, 4)
        for slot_, z in ((0, mz), (1, side), (2, side + 1), (3, 2 * lax.rem(zp + 2, 4) + 1 - i))[kinds]:
            remote(rsend.at[4 * q + slot_], rrecv.at[me // 2], RS, sems.at[RR], column + z, f).start()

    def pair_sum(g):
        span = pl.ds(pl.multiple_of(16 * g, 16), 16)
        wait(precv.at[pl.ds(0, 16)], p_sem.at[g])
        own = rows32[pl.ds(pl.multiple_of(768 * g, 768), 768), :].astype(BF16).astype(F32)
        other = precv[span].reshape(768, 128).astype(F32)
        rsend[span] = (own + other).astype(BF16).reshape(16, 48, 128)

    def back_column(q, carry):
        send_back(q, slice(0, 4))
        return carry

    pair_sum(0)
    own_r = pltpu.make_async_copy(rsend.at[0], rrecv.at[me // 2], sems.at[RR])
    own_r.start()
    send_back(0, slice(1, 4))
    lax.fori_loop(1, 4, back_column, 0)

    def back_group(g, carry):
        pair_sum(g)
        lax.fori_loop(4 * g, 4 * g + 4, back_column, 0)
        return carry

    lax.fori_loop(1, 4, back_group, 0)
    wait(rrecv, sems.at[RR])

    def widen_back(b, carry):
        rows32[pl.ds(pl.multiple_of(384 * b, 384), 384), :] = (
            rrecv[pl.ds(pl.multiple_of(8 * b, 8), 8)].reshape(384, 128).astype(F32)
        )
        return carry

    lax.fori_loop(0, 8, widen_back, 0)
    for c in range(4):
        ybuf[:, 128 * c : 128 * (c + 1)] = rows32[pl.ds(c, 768, stride=4), :].astype(BF16)
    total = jnp.dot(comb_hi[...], ybuf[...], preferred_element_type=F32)
    total = total + jnp.dot(comb_lo[...], ybuf[...], preferred_element_type=F32)
    for s in range(2):
        cols = slice(256 * s, 256 * (s + 1))
        mine_o = obuf[2 * f + s]
        att_ref[:, cols] = mine_o
        summed = hid_ref[:, cols].astype(F32) + mine_o.astype(F32)
        mix_ref[:, cols] = (summed + total[:, cols]).astype(BF16)

    wait(qsend, sems.at[QS])
    wait(kvr.at[pl.ds(0, N - 1)], sems.at[KVS])
    wait(hbuf.at[pl.ds(0, 2)], sems.at[HS])
    wait(hbuf.at[0], sems.at[HFS])
    wait(gbuf.at[pl.ds(0, 3)], sems.at[GS])
    wait(obuf.at[pl.ds(0, 7)], sems.at[OS])
    wait(rrecv.at[pl.ds(0, 63)], sems.at[DS])
    wait(drecv.at[0], sems.at[FS])
    wait(precv, sems.at[PS])
    wait(rrecv.at[pl.ds(0, 63)], sems.at[RS])
    for s in (WS, WT, WFS):
        wait(wg.at[early], sems.at[s])
    for s in (US, UT, UFS):
        wait(wg.at[late], sems.at[s])
    for half in range(2):
        for s in range(3):
            wait(abuf.at[half, 0], sems.at[30 + 6 * half + s])


def per_device(
    hidden_state_stream,
    question_vectors,
    memory_lookup_vectors,
    content_vectors,
    logit_multiplier,
    chosen_tile_lists,
    premix_rmsnorm_scaling,
    routing_choice_ids,
    routing_shares,
    gating_matrix,
    raising_matrix,
    lowering_matrix,
):
    src = (chosen_tile_lists[:, :, None] * 4 + jnp.arange(4, dtype=jnp.int32)).reshape(1, 1024)
    gain = jnp.broadcast_to(premix_rmsnorm_scaling[None, :], (8, 512))
    vmem = pl.BlockSpec(memory_space=pltpu.VMEM)
    hbm = pl.BlockSpec(memory_space=pl.ANY)
    scratch = [
        pltpu.VMEM((64, 2, 32, 256), BF16),
        pltpu.VMEM((N, 32, 256), BF16),
        pltpu.VMEM((2, 256, 256), BF16),
        pltpu.VMEM((256, 256), BF16),
        pltpu.VMEM((4, 256, 512), BF16),
        pltpu.VMEM((4, 8, 512), F32),
        pltpu.VMEM((8, 256, 256), BF16),
        pltpu.VMEM((2, 256, 256), BF16),
        pltpu.VMEM((2, 2, 256, 128), F32),
        pltpu.VMEM((2, 2, 256, 128), F32),
        pltpu.VMEM((192, 256), BF16),
        pltpu.VMEM((256, 768), BF16),
        pltpu.VMEM((256, 768), BF16),
        pltpu.VMEM((3072, 128), F32),
        pltpu.VMEM((64, 48, 128), BF16),
        pltpu.VMEM((2, 64, 48, 128), BF16),
        pltpu.VMEM((192, 2048), BF16),
        pltpu.VMEM((2, 4, 192, 704), BF16),
        pltpu.VMEM((64, 48, 128), BF16),
        pltpu.VMEM((64, 48, 128), BF16),
        pltpu.VMEM((64, 48, 128), BF16),
        pltpu.VMEM((64, 48, 128), BF16),
        pltpu.VMEM((768, 512), BF16),
        pltpu.VMEM((704, 2048), BF16),
        pltpu.VMEM((704, 2048), BF16),
        pltpu.VMEM((704, 512), BF16),
        pltpu.SemaphoreType.DMA((40,)),
        pltpu.SemaphoreType.DMA((GROUPS,)),
        pltpu.SemaphoreType.DMA((4,)),
        pltpu.SemaphoreType.DMA((4,)),
        pltpu.SemaphoreType.DMA((4,)),
        pltpu.SemaphoreType.DMA((2, 3)),
    ]
    shape = jax.ShapeDtypeStruct((256, 512), BF16)
    return pl.pallas_call(
        layer_kernel,
        out_shape=(shape, shape),
        in_specs=[pl.BlockSpec(memory_space=pltpu.SMEM)] + [vmem] * 8 + [hbm] * 3,
        out_specs=(vmem, vmem),
        scratch_shapes=scratch,
        name="layer",
        cost_estimate=pl.CostEstimate(flops=5_000_000_000, bytes_accessed=20_000_000, transcendentals=3_000_000),
        compiler_params=pltpu.CompilerParams(
            collective_id=1, has_side_effects=True, vmem_limit_bytes=52 * 2**20
        ),
    )(
        logit_multiplier,
        hidden_state_stream,
        question_vectors,
        memory_lookup_vectors.reshape(256, 512),
        content_vectors.reshape(256, 512),
        src,
        gain,
        routing_choice_ids.T,
        routing_shares.T,
        gating_matrix,
        raising_matrix,
        lowering_matrix,
    )


def solution(mesh):
    in_specs = (
        P("ctx", "exp"),
        P("ctx", "exp"),
        P(None, "ctx", "exp"),
        P(None, "ctx", "exp"),
        P("exp"),
        P(),
        P("exp"),
        P("ctx", None),
        P("ctx", None),
        P("ctx", "exp", None),
        P("ctx", "exp", None),
        P("ctx", None, "exp"),
    )
    out_specs = (P("ctx", "exp"), P("ctx", "exp"))
    return jax.shard_map(
        per_device, mesh=mesh, in_specs=in_specs, out_specs=out_specs, check_vma=False
    )
```

```python
import functools
import math

import jax
import jax.numpy as jnp
from jax import lax
from jax.experimental import pallas as pl
from jax.experimental.pallas import tpu as pltpu
from jax.sharding import PartitionSpec as P

D = 2048
EXPERTS = 64
CAP = 12
N = 128
OWN = 40
MESH = pl.DeviceIdType.MESH
F32 = jnp.float32
BF16 = jnp.bfloat16

NT = (((1,), (1,)), ((), ()))


def unit_heads(x):
    parts = []
    for h in range(x.shape[1] // 128):
        s = x[:, 128 * h : 128 * (h + 1)].astype(F32)
        parts.append(s * lax.rsqrt(jnp.mean(s * s, axis=1, keepdims=True) + 1e-06))
    return jnp.concatenate(parts, axis=1).astype(BF16)


def layer_kernel(
    mult_ref,
    hid_ref,
    q_ref,
    k_ref,
    v_ref,
    src_ref,
    gain_ref,
    ids_ref,
    share_ref,
    gate_ref,
    up_ref,
    down_ref,
    att_ref,
    mix_ref,
    kvs,
    mid_a,
    mid_b,
    kvr_a,
    kvr_b,
    qbuf,
    qsend,
    hbuf,
    gbuf,
    obuf,
    osend,
    acc,
    den,
    disp,
    comb_hi,
    comb_lo,
    rows32,
    part32,
    dsend,
    drecv,
    xbuf,
    abuf_a,
    abuf_b,
    psend,
    precv,
    rsend,
    rrecv,
    ybuf,
    wg,
    wu,
    wd,
    sems,
    kva_sem,
    kvb_sem,
    d_sem,
    ds_sem,
    fwd_sem,
    p_sem,
    a_sem,
):
    me = lax.axis_index("ctx")
    f = lax.axis_index("exp")
    i = lax.rem(me, 2)
    nb = me + 1 - 2 * i
    f1 = f + 1 - 2 * lax.rem(f, 2)
    f2 = lax.rem(f + 2, 4)
    f3 = 3 - f
    mz = lax.rem(me, 8)
    my = lax.rem(me // 8, 8)
    mx = me // 64
    zp = mz // 2
    xy = me // 8
    (QS, QR, HS, HX, HC, HF, HFS, GS, GR, OS, OR, DS, FS, PS, RS, RR, OX, OY, OZ, OFS, K1, K2, K3, K4, KA, KB, KL, KM) = range(16 + 12)
    (WS, WX, WT, WC, WF, WFS, US, UX, UT, UC, UF, UFS, LOCW) = range(28, 41)
    AS = 41

    bar = pltpu.get_barrier_semaphore()

    def greet(k, carry):
        pl.semaphore_signal(bar, inc=1, device_id=(lax.rem(me + k, N), f), device_id_type=MESH)
        return carry

    lax.fori_loop(1, N, greet, 0)
    for g in (f1, f2, f3):
        pl.semaphore_signal(bar, inc=1, device_id=(me, g), device_id_type=MESH)
        pl.semaphore_signal(bar, inc=1, device_id=(nb, g), device_id_type=MESH)

    pick = (lax.broadcasted_iota(jnp.int32, (256, 1024), 0) == src_ref[...]).astype(F32)
    pick = jnp.transpose(pick).astype(BF16)
    kunit = unit_heads(k_ref[...])
    for half in range(2):
        for head in range(2):
            cols = slice(256 * half + 128 * head, 256 * half + 128 * head + 128)
            got = jnp.dot(pick, kunit[:, cols], preferred_element_type=F32).astype(BF16)
            kvs[:, :, half, head, 0:16, :] = got.reshape(16, 4, 16, 128)
            got = jnp.dot(pick, v_ref[:, cols], preferred_element_type=F32).astype(BF16)
            kvs[:, :, half, head, 16:32, :] = got.reshape(16, 4, 16, 128)

    pl.semaphore_wait(bar, N - 1 + 6)

    def remote(src, dst, s, r, ctx, ex):
        left = sems.at[s] if isinstance(s, int) else s
        return pltpu.make_async_remote_copy(
            src, dst, left, r, device_id=(ctx, ex), device_id_type=MESH
        )

    def wait(ref, sem):
        pltpu.make_async_copy(ref, ref, sem).wait()

    def ring(k):
        return xy * 8 + lax.rem(mz + k, 8)

    def column(k):
        return lax.rem(xy + k, 16) * 8 + mz

    def first_z(k):
        d = lax.rem(mz + k, 8)
        src = kvs.at[:, d // 2, lax.rem(d, 2), 0]
        remote(src, mid_a.at[mz], K3, sems.at[KA], ring(k), f).start()

    def first_xy(k):
        d = lax.rem(xy + k, 16)
        remote(kvs.at[d, :, :, 1], mid_b.at[xy], K1, sems.at[KB], column(k), f).start()

    def first_step(k, carry):
        first_z(k)
        first_xy(2 * k - 1)
        first_xy(2 * k)
        return carry

    lax.fori_loop(1, 8, first_step, 0)
    first_xy(15)
    own_a = pltpu.make_async_copy(kvs.at[:, mz // 2, lax.rem(mz, 2), 0], mid_a.at[mz], sems.at[KM])
    own_a.start()
    own_b = pltpu.make_async_copy(kvs.at[xy, :, :, 1], mid_b.at[xy], sems.at[KL])
    own_b.start()

    def shard(who, lo, hi):
        return pl.ds(pl.multiple_of(who * 176 + lo, 16), hi - lo)

    for g, left, sem in ((f2, WS, WX), (f1, WT, WC)):
        remote(gate_ref.at[0], wg.at[shard(f, 0, 176)], left, sems.at[sem], me, g).start()
    for c in (
        pltpu.make_async_copy(gate_ref.at[0], wg.at[shard(f, 0, 176)], sems.at[LOCW]),
        pltpu.make_async_copy(up_ref.at[0], wu.at[shard(f, 0, 176)], sems.at[LOCW]),
        pltpu.make_async_copy(down_ref.at[0], wd, sems.at[LOCW]),
    ):
        c.start()

    qunit = unit_heads(q_ref[...])
    first = jnp.broadcast_to(i, (256, 256)) == 0
    qbuf[i] = jnp.where(first, qunit[:, :256], qunit[:, 256:])
    qsend[...] = jnp.where(first, qunit[:, 256:], qunit[:, :256])
    remote(qsend, qbuf.at[i], QS, sems.at[QR], nb, f).start()

    for g, sem in ((f2, HX), (f1, HC)):
        remote(hid_ref, hbuf.at[f], HS, sems.at[sem], me, g).start()
    for g in (f1, f2, f3):
        remote(gain_ref, gbuf.at[f], GS, sems.at[GR], me, g).start()
    hbuf[f] = hid_ref[...]
    gbuf[f] = gain_ref[...]

    ids = ids_ref[...]
    experts = lax.broadcasted_iota(jnp.int32, (EXPERTS, 256), 0)
    named = [(experts == ids[c : c + 1, :]).astype(F32) for c in range(2)]
    counts = (named[0] + named[1]).astype(BF16)
    earlier = (
        lax.broadcasted_iota(jnp.int32, (256, 256), 0) < lax.broadcasted_iota(jnp.int32, (256, 256), 1)
    ).astype(F32).astype(BF16)
    before = jnp.dot(counts, earlier, preferred_element_type=F32)
    keys = []
    for c in range(2):
        rank = jnp.sum(named[c] * before, axis=0, keepdims=True)
        keys.append(ids[c : c + 1, :] * CAP + rank.astype(jnp.int32))
    row = lax.broadcasted_iota(jnp.int32, (192, 256), 0)
    expert = (row * 171) // 512
    slot = expert * CAP + (row - expert * 3)
    mine = slot + 3 * f
    disp[...] = ((keys[0] == mine) | (keys[1] == mine)).astype(F32).astype(BF16)
    for b in range(3):
        line = lax.broadcasted_iota(jnp.int32, (256, 256), 0) + 256 * b
        expert = (line * 5462) // 65536
        inner = line - expert * 12
        there = expert * CAP + 3 * lax.rem(inner, 4) + inner // 4
        table = jnp.where(keys[0] == there, share_ref[0:1, :], 0.0) + jnp.where(
            keys[1] == there, share_ref[1:2, :], 0.0
        )
        high = table.astype(BF16).astype(F32)
        comb_hi[:, 256 * b : 256 * (b + 1)] = jnp.transpose(high).astype(BF16)
        comb_lo[:, 256 * b : 256 * (b + 1)] = jnp.transpose(table - high).astype(BF16)

    own_a.wait()
    own_b.wait()
    wait(mid_a.at[pl.ds(0, 7)], sems.at[KA])
    own_a = pltpu.make_async_copy(mid_a.at[:, xy], kvr_a.at[0], kva_sem.at[0])
    own_a.start()

    def second_xy(k, carry):
        d = lax.rem(xy + k, 16)
        remote(mid_a.at[:, d], kvr_a.at[k], K2, kva_sem.at[k // 4], column(k), f).start()
        return carry

    lax.fori_loop(1, 16, second_xy, 0)
    wait(mid_b.at[pl.ds(0, 15)], sems.at[KB])
    own_b = pltpu.make_async_copy(mid_b.at[:, mz // 2, lax.rem(mz, 2)], kvr_b.at[0], kvb_sem.at[0])
    own_b.start()

    def second_z(k, carry):
        d = lax.rem(mz + k, 8)
        remote(
            mid_b.at[:, d // 2, lax.rem(d, 2)], kvr_b.at[k], K4, kvb_sem.at[k // 2], ring(k), f
        ).start()
        return carry

    lax.fori_loop(1, 8, second_z, 0)

    acc[...] = jnp.zeros_like(acc)
    den[...] = jnp.zeros_like(den)
    wait(qbuf.at[0], sems.at[QR])

    def attend(h, kg, vg):
        cols = slice(128 * h, 128 * (h + 1))
        scale = mult_ref[2 * i + h] * (1.0 / math.sqrt(128.0))
        for j in range(2):
            s = lax.dot_general(qbuf[j, :, cols], kg, NT, preferred_element_type=F32)
            e = jnp.exp(s * scale)
            total = e[:, 0:128]
            for c in range(1, 4):
                total = total + e[:, 128 * c : 128 * (c + 1)]
            den[j, h] += total
            acc[j, h] += jnp.dot(e.astype(BF16), vg, preferred_element_type=F32)

    def attend_group(g, carry):
        wait(kvr_a.at[pl.ds(0, 4)], kva_sem.at[g])
        span = pl.ds(pl.multiple_of(4 * g, 4), 4)
        attend(0, kvr_a[span, :, 0:16, :].reshape(512, 128), kvr_a[span, :, 16:32, :].reshape(512, 128))
        wait(kvr_b.at[pl.ds(0, 2)], kvb_sem.at[g])
        span = pl.ds(pl.multiple_of(2 * g, 2), 2)
        attend(1, kvr_b[span, :, 0:16, :].reshape(512, 128), kvr_b[span, :, 16:32, :].reshape(512, 128))
        return carry

    lax.fori_loop(0, 4, attend_group, 0)
    for j in range(2):
        for h in range(2):
            out = acc[j, h] / jnp.sum(den[j, h], axis=1, keepdims=True)
            osend[j, :, 128 * h : 128 * (h + 1)] = out.astype(BF16)

    wait(hbuf.at[0], sems.at[HX])
    remote(hbuf.at[f2], hbuf.at[f2], HFS, sems.at[HF], me, f1).start()
    mark = 2 * f + i
    for src, ctx, sem in ((i, me, OX), (1 - i, nb, OY)):
        remote(osend.at[src], obuf.at[mark], OS, sems.at[sem], ctx, f2).start()
    remote(osend.at[1 - i], obuf.at[mark], OS, sems.at[OZ], nb, f).start()
    remote(osend.at[i], obuf.at[mark], OS, sems.at[OR], me, f1).start()
    obuf[mark] = osend[i]
    for who, sem in ((2 * f + 1 - i, OZ), (2 * f2 + i, OX), (2 * f2 + 1 - i, OY)):
        wait(obuf.at[0], sems.at[sem])
        remote(obuf.at[who], obuf.at[who], OFS, sems.at[OR], me, f1).start()
    early = pl.ds(0, 176)
    wait(wg.at[early], sems.at[WX])
    remote(wg.at[shard(f2, 0, 176)], wg.at[shard(f2, 0, 176)], WFS, sems.at[WF], me, f1).start()
    wait(hbuf.at[0], sems.at[HC])
    wait(hbuf.at[0], sems.at[HF])
    wait(gbuf.at[pl.ds(0, 3)], sems.at[GR])
    wait(obuf.at[pl.ds(0, 4)], sems.at[OR])

    for g, left, sem in ((f2, US, UX), (f1, UT, UC)):
        remote(up_ref.at[0], wu.at[shard(f, 0, 176)], left, sems.at[sem], me, g).start()

    squares = jnp.zeros((256, 1), F32)
    for s in range(8):
        cols = slice(256 * (s % 2), 256 * (s % 2) + 256)
        part = hbuf[s // 2, :, cols].astype(F32) + obuf[s].astype(F32)
        squares = squares + jnp.sum(part * part, axis=1, keepdims=True)
    inverse = lax.rsqrt(squares / D + 1e-05)
    for s in range(8):
        cols = slice(256 * (s % 2), 256 * (s % 2) + 256)
        part = hbuf[s // 2, :, cols].astype(F32) + obuf[s].astype(F32)
        unit = (part * inverse * gbuf[s // 2, 0:1, cols]).astype(BF16)
        sent = jnp.dot(disp[...], unit, preferred_element_type=F32)
        for c in range(2):
            rows32[pl.ds(2 * s + c, 192, stride=16), :] = sent[:, 128 * c : 128 * (c + 1)]
    for b in range(8):
        dsend[pl.ds(8 * b, 8)] = rows32[pl.ds(384 * b, 384), :].astype(BF16).reshape(8, 48, 128)

    steps = ((3, 5), (2, 6), (4, 0), (1, 7))

    def near(g, m, sign):
        low, high = steps[g]
        x = lax.rem(mx + m, 2)
        y = lax.rem(my + 8 + sign * (low + (high - low) * (m // 2)), 8)
        return x * 64 + y * 8

    def send_rows(g, m, kinds):
        column_ = near(g, m, 1)
        for off, member, slot_ in (
            (0, i, 0),
            (1, 0, 1 + i),
            (3, 1, 1 + i),
            (2, 1 - i, 3),
        )[kinds]:
            pair = lax.rem(zp + off, 4)
            remote(
                dsend.at[column_ // 2 + pair],
                drecv.at[1, 16 * g + 4 * m + slot_],
                ds_sem.at[g],
                d_sem.at[g],
                column_ + 2 * pair + member,
                f,
            ).start()

    def send_group(g, each):
        def one(m, carry):
            each(g, m, slice(0, 4))
            return carry

        if 0 in steps[g]:
            lax.fori_loop(0, 2, one, 0)
            each(g, 2, slice(1, 4))
            each(g, 3, slice(0, 4))
        else:
            lax.fori_loop(0, 4, one, 0)

    own_d = pltpu.make_async_copy(dsend.at[me // 2], drecv.at[1, OWN], d_sem.at[OWN // 16])
    own_d.start()
    send_group(0, send_rows)
    send_group(1, send_rows)
    for g in range(4):
        span = pl.ds(16 * g, 16)
        wait(drecv.at[1, span], d_sem.at[g])
        remote(drecv.at[1, span], drecv.at[0, span], FS, fwd_sem.at[g], nb, f).start()
        if g < 2:
            wait(drecv.at[1, pl.ds(0, 16)], ds_sem.at[g])
            send_group(g + 2, send_rows)

    wait(wg.at[early], sems.at[UX])
    remote(wu.at[shard(f2, 0, 176)], wu.at[shard(f2, 0, 176)], UFS, sems.at[UF], me, f1).start()
    wait(wg.at[pl.ds(0, 528)], sems.at[LOCW])
    wait(wg.at[early], sems.at[WC])
    wait(wg.at[early], sems.at[WF])
    wait(wg.at[early], sems.at[UC])
    wait(wg.at[early], sems.at[UF])

    def hidden(part_, kind, first_slot, rows, mine_buf):
        def widen(b, carry):
            rows32[pl.ds(pl.multiple_of(384 * b, 384), 384), :] = (
                drecv[kind, pl.ds(pl.multiple_of(first_slot + 8 * b, 8), 8)].reshape(384, 128).astype(F32)
            )
            return carry

        lax.fori_loop(0, rows // 24, widen, 0)
        for c in range(16):
            xbuf[0:rows, 128 * c : 128 * (c + 1)] = rows32[pl.ds(c, rows, stride=16), :].astype(BF16)
        x = xbuf[0:rows, :]
        for lo, hi in ((0, 256), (256, 512), (512, 704)):
            gate = lax.dot_general(x, wg[lo:hi, :], NT, preferred_element_type=F32)
            up = lax.dot_general(x, wu[lo:hi, :], NT, preferred_element_type=F32)
            mine_buf[f, :, lo:hi] = (gate / (1.0 + jnp.exp(-gate)) * up).astype(BF16)
        here = mine_buf.at[f]
        remote(here, here, AS + 3 * part_, a_sem.at[part_, 0], me, f2).start()
        remote(here, here, AS + 3 * part_ + 1, a_sem.at[part_, 1], me, f1).start()

    def share_on(part_, buf):
        wait(buf.at[0], a_sem.at[part_, 0])
        remote(buf.at[f2], buf.at[f2], AS + 3 * part_ + 2, a_sem.at[part_, 2], me, f1).start()

    def lower(part_, buf, rows, out32):
        for s in (1, 2):
            wait(buf.at[0], a_sem.at[part_, s])
        for g in range(4):
            out = jnp.dot(buf[g], wd[...], preferred_element_type=F32)
            for c in range(4):
                out32[pl.ds(4 * g + c, rows, stride=16), :] = out[:, 128 * c : 128 * (c + 1)]

    def partner(first_group):
        for g in range(2):
            span = pl.ds(16 * (first_group + g), 16)
            psend[span] = part32[768 * g : 768 * (g + 1), :].astype(BF16).reshape(16, 48, 128)
            remote(psend.at[span], precv.at[span], PS, p_sem.at[first_group + g], nb, f).start()

    part_b, part_c = abuf_b.at[0], abuf_b.at[1]
    hidden(0, 1, 0, 192, abuf_a)
    for g in range(2):
        wait(drecv.at[0, pl.ds(0, 16)], fwd_sem.at[g])
    hidden(1, 0, 0, 96, part_b)
    share_on(0, abuf_a)
    share_on(1, part_b)
    for g in range(2, 4):
        wait(drecv.at[0, pl.ds(0, 16)], fwd_sem.at[g])
    hidden(2, 0, 32, 96, part_c)
    lower(1, part_b, 96, part32)
    partner(0)
    lower(0, abuf_a, 192, rows32)
    share_on(2, part_c)
    lower(2, part_c, 96, part32)
    partner(2)

    def send_back(g, m, kinds):
        column_ = near(g, m, -1)
        side = 2 * lax.rem(zp + 3 + 2 * i, 4)
        for slot_, z in ((0, mz), (1, side), (2, side + 1), (3, 2 * lax.rem(zp + 2, 4) + 1 - i))[kinds]:
            remote(
                rsend.at[16 * g + 4 * m + slot_], rrecv.at[me // 2], RS, sems.at[RR], column_ + z, f
            ).start()

    for g in range(4):
        span = pl.ds(16 * g, 16)
        wait(precv.at[span], p_sem.at[g])
        own = rows32[768 * g : 768 * (g + 1), :].astype(BF16).astype(F32)
        other = precv[span].reshape(768, 128).astype(F32)
        rsend[span] = (own + other).astype(BF16).reshape(16, 48, 128)
        if g == OWN // 16:
            own_r = pltpu.make_async_copy(rsend.at[OWN], rrecv.at[me // 2], sems.at[RR])
            own_r.start()
        send_group(g, send_back)
    wait(rrecv, sems.at[RR])

    def widen_back(b, carry):
        rows32[pl.ds(pl.multiple_of(384 * b, 384), 384), :] = (
            rrecv[pl.ds(pl.multiple_of(8 * b, 8), 8)].reshape(384, 128).astype(F32)
        )
        return carry

    lax.fori_loop(0, 8, widen_back, 0)
    for c in range(4):
        ybuf[:, 128 * c : 128 * (c + 1)] = rows32[pl.ds(c, 768, stride=4), :].astype(BF16)
    total = jnp.dot(comb_hi[...], ybuf[...], preferred_element_type=F32)
    total = total + jnp.dot(comb_lo[...], ybuf[...], preferred_element_type=F32)
    for s in range(2):
        cols = slice(256 * s, 256 * (s + 1))
        mine_o = obuf[2 * f + s]
        att_ref[:, cols] = mine_o
        summed = hid_ref[:, cols].astype(F32) + mine_o.astype(F32)
        mix_ref[:, cols] = (summed + total[:, cols]).astype(BF16)

    wait(qsend, sems.at[QS])
    wait(kvr_a.at[pl.ds(0, 15)], sems.at[K1])
    wait(kvr_a.at[pl.ds(0, 15)], sems.at[K2])
    wait(kvr_b.at[pl.ds(0, 7)], sems.at[K3])
    wait(kvr_b.at[pl.ds(0, 7)], sems.at[K4])
    wait(hbuf.at[pl.ds(0, 2)], sems.at[HS])
    wait(hbuf.at[0], sems.at[HFS])
    wait(gbuf.at[pl.ds(0, 3)], sems.at[GS])
    wait(obuf.at[pl.ds(0, 4)], sems.at[OS])
    wait(obuf.at[pl.ds(0, 3)], sems.at[OFS])
    wait(rrecv.at[pl.ds(0, 15)], ds_sem.at[2])
    wait(rrecv.at[pl.ds(0, 16)], ds_sem.at[3])
    wait(drecv.at[0], sems.at[FS])
    wait(precv, sems.at[PS])
    wait(rrecv.at[pl.ds(0, 63)], sems.at[RS])
    for s in (WS, WT, WFS):
        wait(wg.at[early], sems.at[s])
    for s in (US, UT, UFS):
        wait(wg.at[early], sems.at[s])
    for s in range(3):
        wait(abuf_a.at[0], sems.at[AS + s])
        wait(abuf_b.at[0, 0], sems.at[AS + 3 + s])
        wait(abuf_b.at[0, 0], sems.at[AS + 6 + s])


def per_device(
    hidden_state_stream,
    question_vectors,
    memory_lookup_vectors,
    content_vectors,
    logit_multiplier,
    chosen_tile_lists,
    premix_rmsnorm_scaling,
    routing_choice_ids,
    routing_shares,
    gating_matrix,
    raising_matrix,
    lowering_matrix,
):
    src = (chosen_tile_lists[:, :, None] * 4 + jnp.arange(4, dtype=jnp.int32)).reshape(1, 1024)
    gain = jnp.broadcast_to(premix_rmsnorm_scaling[None, :], (8, 512))
    vmem = pl.BlockSpec(memory_space=pltpu.VMEM)
    hbm = pl.BlockSpec(memory_space=pl.ANY)
    scratch = [
        pltpu.VMEM((16, 4, 2, 2, 32, 128), BF16),
        pltpu.VMEM((8, 16, 32, 128), BF16),
        pltpu.VMEM((16, 4, 2, 32, 128), BF16),
        pltpu.VMEM((16, 8, 32, 128), BF16),
        pltpu.VMEM((8, 16, 32, 128), BF16),
        pltpu.VMEM((2, 256, 256), BF16),
        pltpu.VMEM((256, 256), BF16),
        pltpu.VMEM((4, 256, 512), BF16),
        pltpu.VMEM((4, 8, 512), F32),
        pltpu.VMEM((8, 256, 256), BF16),
        pltpu.VMEM((2, 256, 256), BF16),
        pltpu.VMEM((2, 2, 256, 128), F32),
        pltpu.VMEM((2, 2, 256, 128), F32),
        pltpu.VMEM((192, 256), BF16),
        pltpu.VMEM((256, 768), BF16),
        pltpu.VMEM((256, 768), BF16),
        pltpu.VMEM((3072, 128), F32),
        pltpu.VMEM((1536, 128), F32),
        pltpu.VMEM((64, 48, 128), BF16),
        pltpu.VMEM((2, 64, 48, 128), BF16),
        pltpu.VMEM((192, 2048), BF16),
        pltpu.VMEM((4, 192, 704), BF16),
        pltpu.VMEM((2, 4, 96, 704), BF16),
        pltpu.VMEM((64, 48, 128), BF16),
        pltpu.VMEM((64, 48, 128), BF16),
        pltpu.VMEM((64, 48, 128), BF16),
        pltpu.VMEM((64, 48, 128), BF16),
        pltpu.VMEM((768, 512), BF16),
        pltpu.VMEM((704, 2048), BF16),
        pltpu.VMEM((704, 2048), BF16),
        pltpu.VMEM((704, 512), BF16),
        pltpu.SemaphoreType.DMA((50,)),
        pltpu.SemaphoreType.DMA((4,)),
        pltpu.SemaphoreType.DMA((4,)),
        pltpu.SemaphoreType.DMA((4,)),
        pltpu.SemaphoreType.DMA((4,)),
        pltpu.SemaphoreType.DMA((4,)),
        pltpu.SemaphoreType.DMA((4,)),
        pltpu.SemaphoreType.DMA((3, 3)),
    ]
    shape = jax.ShapeDtypeStruct((256, 512), BF16)
    return pl.pallas_call(
        layer_kernel,
        out_shape=(shape, shape),
        in_specs=[pl.BlockSpec(memory_space=pltpu.SMEM)] + [vmem] * 8 + [hbm] * 3,
        out_specs=(vmem, vmem),
        scratch_shapes=scratch,
        name="layer",
        cost_estimate=pl.CostEstimate(flops=5_000_000_000, bytes_accessed=20_000_000, transcendentals=3_000_000),
        compiler_params=pltpu.CompilerParams(
            collective_id=1, has_side_effects=True, vmem_limit_bytes=52 * 2**20
        ),
    )(
        logit_multiplier,
        hidden_state_stream,
        question_vectors,
        memory_lookup_vectors.reshape(256, 512),
        content_vectors.reshape(256, 512),
        src,
        gain,
        routing_choice_ids.T,
        routing_shares.T,
        gating_matrix,
        raising_matrix,
        lowering_matrix,
    )


def solution(mesh):
    in_specs = (
        P("ctx", "exp"),
        P("ctx", "exp"),
        P(None, "ctx", "exp"),
        P(None, "ctx", "exp"),
        P("exp"),
        P(),
        P("exp"),
        P("ctx", None),
        P("ctx", None),
        P("ctx", "exp", None),
        P("ctx", "exp", None),
        P("ctx", None, "exp"),
    )
    out_specs = (P("ctx", "exp"), P("ctx", "exp"))
    return jax.shard_map(
        per_device, mesh=mesh, in_specs=in_specs, out_specs=out_specs, check_vma=False
    )
```

```python
import functools
import math

import jax
import jax.numpy as jnp
from jax import lax
from jax.experimental import pallas as pl
from jax.experimental.pallas import tpu as pltpu
from jax.sharding import PartitionSpec as P

D = 2048
EXPERTS = 64
CAP = 12
N = 128
OWN = 40
MESH = pl.DeviceIdType.MESH
F32 = jnp.float32
BF16 = jnp.bfloat16

NT = (((1,), (1,)), ((), ()))


def unit_heads(x):
    parts = []
    for h in range(x.shape[1] // 128):
        s = x[:, 128 * h : 128 * (h + 1)].astype(F32)
        parts.append(s * lax.rsqrt(jnp.mean(s * s, axis=1, keepdims=True) + 1e-06))
    return jnp.concatenate(parts, axis=1).astype(BF16)


def layer_kernel(
    mult_ref,
    hid_ref,
    q_ref,
    k_ref,
    v_ref,
    src_ref,
    gain_ref,
    ids_ref,
    share_ref,
    gate_ref,
    up_ref,
    down_ref,
    att_ref,
    mix_ref,
    kvs,
    mid_a,
    mid_b,
    kvr_a,
    kvr_b,
    qown,
    qbuf,
    qsend,
    hbuf,
    gbuf,
    obuf,
    osend,
    acc,
    den,
    disp,
    comb_hi,
    comb_lo,
    rows32,
    part32,
    wide32,
    dsend,
    drecv,
    xbuf,
    abuf_a,
    abuf_b,
    psend,
    precv,
    rsend,
    rrecv,
    ybuf,
    wg,
    wu,
    wd,
    sems,
    kva_sem,
    kvb_sem,
    d_sem,
    ds_sem,
    fwd_sem,
    p_sem,
    a_sem,
    in_sem,
):
    me = lax.axis_index("ctx")
    f = lax.axis_index("exp")
    i = lax.rem(me, 2)
    nb = me + 1 - 2 * i
    f1 = f + 1 - 2 * lax.rem(f, 2)
    f2 = lax.rem(f + 2, 4)
    f3 = 3 - f
    mz = lax.rem(me, 8)
    my = lax.rem(me // 8, 8)
    mx = me // 64
    zp = mz // 2
    xy = me // 8
    (QS, QR, HS, HX, HC, HF, HFS, GS, GR, OS, OR, DS, FS, PS, RS, RR, OX, OY, OZ, OFS, K1, K2, K3, K4, KA, KB, KL, KM) = range(16 + 12)
    (WS, WX, WT, WC, WF, WFS, US, UX, UT, UC, UF, UFS, LOCW) = range(28, 41)
    AS = 41

    own_q = pltpu.make_async_copy(q_ref, qown, in_sem.at[0])
    own_q.start()
    own_h = pltpu.make_async_copy(hid_ref, hbuf.at[f], in_sem.at[1])
    own_h.start()

    bar = pltpu.get_barrier_semaphore()

    def greet(k, carry):
        pl.semaphore_signal(bar, inc=1, device_id=(lax.rem(me + k, N), f), device_id_type=MESH)
        return carry

    lax.fori_loop(1, N, greet, 0)
    for g in (f1, f2, f3):
        pl.semaphore_signal(bar, inc=1, device_id=(me, g), device_id_type=MESH)
        pl.semaphore_signal(bar, inc=1, device_id=(nb, g), device_id_type=MESH)

    pick = (lax.broadcasted_iota(jnp.int32, (256, 1024), 0) == src_ref[...]).astype(F32)
    pick = jnp.transpose(pick).astype(BF16)
    kunit = unit_heads(k_ref[...])
    for half in range(2):
        for head in range(2):
            cols = slice(256 * half + 128 * head, 256 * half + 128 * head + 128)
            got = jnp.dot(pick, kunit[:, cols], preferred_element_type=F32).astype(BF16)
            kvs[:, :, half, head, 0:16, :] = got.reshape(16, 4, 16, 128)
            got = jnp.dot(pick, v_ref[:, cols], preferred_element_type=F32).astype(BF16)
            kvs[:, :, half, head, 16:32, :] = got.reshape(16, 4, 16, 128)

    pl.semaphore_wait(bar, N - 1 + 6)

    def remote(src, dst, s, r, ctx, ex):
        left = sems.at[s] if isinstance(s, int) else s
        return pltpu.make_async_remote_copy(
            src, dst, left, r, device_id=(ctx, ex), device_id_type=MESH
        )

    def wait(ref, sem):
        pltpu.make_async_copy(ref, ref, sem).wait()

    def ring(k):
        return xy * 8 + lax.rem(mz + k, 8)

    def column(k):
        return lax.rem(xy + k, 16) * 8 + mz

    def first_z(k):
        d = lax.rem(mz + k, 8)
        src = kvs.at[:, d // 2, lax.rem(d, 2), 0]
        remote(src, mid_a.at[mz], K3, sems.at[KA], ring(k), f).start()

    def first_xy(k):
        d = lax.rem(xy + k, 16)
        remote(kvs.at[d, :, :, 1], mid_b.at[xy], K1, sems.at[KB], column(k), f).start()

    def first_step(k, carry):
        first_z(k)
        first_xy(2 * k - 1)
        first_xy(2 * k)
        return carry

    lax.fori_loop(1, 8, first_step, 0)
    first_xy(15)
    own_a = pltpu.make_async_copy(kvs.at[:, mz // 2, lax.rem(mz, 2), 0], mid_a.at[mz], sems.at[KM])
    own_a.start()
    own_b = pltpu.make_async_copy(kvs.at[xy, :, :, 1], mid_b.at[xy], sems.at[KL])
    own_b.start()

    def shard(who, lo, hi):
        return pl.ds(pl.multiple_of(who * 176 + lo, 16), hi - lo)

    for g, left, sem in ((f2, WS, WX), (f1, WT, WC)):
        remote(gate_ref.at[0], wg.at[shard(f, 0, 176)], left, sems.at[sem], me, g).start()
    for c in (
        pltpu.make_async_copy(gate_ref.at[0], wg.at[shard(f, 0, 176)], sems.at[LOCW]),
        pltpu.make_async_copy(up_ref.at[0], wu.at[shard(f, 0, 176)], sems.at[LOCW]),
        pltpu.make_async_copy(down_ref.at[0], wd, sems.at[LOCW]),
    ):
        c.start()

    own_q.wait()
    own_h.wait()
    qunit = unit_heads(qown[...])
    first = jnp.broadcast_to(i, (256, 256)) == 0
    qbuf[i] = jnp.where(first, qunit[:, :256], qunit[:, 256:])
    qsend[...] = jnp.where(first, qunit[:, 256:], qunit[:, :256])
    remote(qsend, qbuf.at[i], QS, sems.at[QR], nb, f).start()

    for g, sem in ((f2, HX), (f1, HC)):
        remote(hbuf.at[f], hbuf.at[f], HS, sems.at[sem], me, g).start()
    for g in (f1, f2, f3):
        remote(gain_ref, gbuf.at[f], GS, sems.at[GR], me, g).start()
    gbuf[f] = gain_ref[...]

    ids = ids_ref[...]
    experts = lax.broadcasted_iota(jnp.int32, (EXPERTS, 256), 0)
    named = [(experts == ids[c : c + 1, :]).astype(F32) for c in range(2)]
    counts = (named[0] + named[1]).astype(BF16)
    earlier = (
        lax.broadcasted_iota(jnp.int32, (256, 256), 0) < lax.broadcasted_iota(jnp.int32, (256, 256), 1)
    ).astype(F32).astype(BF16)
    before = jnp.dot(counts, earlier, preferred_element_type=F32)
    keys = []
    for c in range(2):
        rank = jnp.sum(named[c] * before, axis=0, keepdims=True)
        keys.append(ids[c : c + 1, :] * CAP + rank.astype(jnp.int32))
    row = lax.broadcasted_iota(jnp.int32, (192, 256), 0)
    expert = (row * 171) // 512
    slot = expert * CAP + (row - expert * 3)
    mine = slot + 3 * f
    disp[...] = ((keys[0] == mine) | (keys[1] == mine)).astype(F32).astype(BF16)
    for b in range(3):
        line = lax.broadcasted_iota(jnp.int32, (256, 256), 0) + 256 * b
        expert = (line * 5462) // 65536
        inner = line - expert * 12
        there = expert * CAP + 3 * lax.rem(inner, 4) + inner // 4
        table = jnp.where(keys[0] == there, share_ref[0:1, :], 0.0) + jnp.where(
            keys[1] == there, share_ref[1:2, :], 0.0
        )
        high = table.astype(BF16).astype(F32)
        comb_hi[:, 256 * b : 256 * (b + 1)] = jnp.transpose(high).astype(BF16)
        comb_lo[:, 256 * b : 256 * (b + 1)] = jnp.transpose(table - high).astype(BF16)

    own_a.wait()
    own_b.wait()
    wait(mid_a.at[pl.ds(0, 7)], sems.at[KA])
    own_a = pltpu.make_async_copy(mid_a.at[:, xy], kvr_a.at[0], kva_sem.at[0])
    own_a.start()

    def second_xy(k, carry):
        d = lax.rem(xy + k, 16)
        remote(mid_a.at[:, d], kvr_a.at[k], K2, kva_sem.at[k // 4], column(k), f).start()
        return carry

    lax.fori_loop(1, 16, second_xy, 0)
    wait(mid_b.at[pl.ds(0, 15)], sems.at[KB])
    own_b = pltpu.make_async_copy(mid_b.at[:, mz // 2, lax.rem(mz, 2)], kvr_b.at[0], kvb_sem.at[0])
    own_b.start()

    def second_z(k, carry):
        d = lax.rem(mz + k, 8)
        remote(
            mid_b.at[:, d // 2, lax.rem(d, 2)], kvr_b.at[k], K4, kvb_sem.at[k // 2], ring(k), f
        ).start()
        return carry

    lax.fori_loop(1, 8, second_z, 0)

    acc[...] = jnp.zeros_like(acc)
    den[...] = jnp.zeros_like(den)
    wait(qbuf.at[0], sems.at[QR])

    def attend(h, kg, vg):
        cols = slice(128 * h, 128 * (h + 1))
        scale = mult_ref[2 * i + h] * (1.0 / math.sqrt(128.0))
        for j in range(2):
            s = lax.dot_general(qbuf[j, :, cols], kg, NT, preferred_element_type=F32)
            e = jnp.exp(s * scale)
            total = e[:, 0:128]
            for c in range(1, 4):
                total = total + e[:, 128 * c : 128 * (c + 1)]
            den[j, h] += total
            acc[j, h] += jnp.dot(e.astype(BF16), vg, preferred_element_type=F32)

    def attend_group(g, carry):
        wait(kvr_a.at[pl.ds(0, 4)], kva_sem.at[g])
        span = pl.ds(pl.multiple_of(4 * g, 4), 4)
        attend(0, kvr_a[span, :, 0:16, :].reshape(512, 128), kvr_a[span, :, 16:32, :].reshape(512, 128))
        wait(kvr_b.at[pl.ds(0, 2)], kvb_sem.at[g])
        span = pl.ds(pl.multiple_of(2 * g, 2), 2)
        attend(1, kvr_b[span, :, 0:16, :].reshape(512, 128), kvr_b[span, :, 16:32, :].reshape(512, 128))
        return carry

    lax.fori_loop(0, 4, attend_group, 0)
    for j in range(2):
        for h in range(2):
            out = acc[j, h] / jnp.sum(den[j, h], axis=1, keepdims=True)
            osend[j, :, 128 * h : 128 * (h + 1)] = out.astype(BF16)

    wait(hbuf.at[0], sems.at[HX])
    remote(hbuf.at[f2], hbuf.at[f2], HFS, sems.at[HF], me, f1).start()
    mark = 2 * f + i
    for src, ctx, sem in ((i, me, OX), (1 - i, nb, OY)):
        remote(osend.at[src], obuf.at[mark], OS, sems.at[sem], ctx, f2).start()
    remote(osend.at[1 - i], obuf.at[mark], OS, sems.at[OZ], nb, f).start()
    remote(osend.at[i], obuf.at[mark], OS, sems.at[OR], me, f1).start()
    obuf[mark] = osend[i]
    for who, sem in ((2 * f + 1 - i, OZ), (2 * f2 + i, OX), (2 * f2 + 1 - i, OY)):
        wait(obuf.at[0], sems.at[sem])
        remote(obuf.at[who], obuf.at[who], OFS, sems.at[OR], me, f1).start()
    early = pl.ds(0, 176)
    wait(wg.at[early], sems.at[WX])
    remote(wg.at[shard(f2, 0, 176)], wg.at[shard(f2, 0, 176)], WFS, sems.at[WF], me, f1).start()
    wait(hbuf.at[0], sems.at[HC])
    wait(hbuf.at[0], sems.at[HF])
    wait(gbuf.at[pl.ds(0, 3)], sems.at[GR])
    wait(obuf.at[pl.ds(0, 4)], sems.at[OR])

    for g, left, sem in ((f2, US, UX), (f1, UT, UC)):
        remote(up_ref.at[0], wu.at[shard(f, 0, 176)], left, sems.at[sem], me, g).start()

    squares = jnp.zeros((256, 1), F32)
    for s in range(8):
        cols = slice(256 * (s % 2), 256 * (s % 2) + 256)
        part = hbuf[s // 2, :, cols].astype(F32) + obuf[s].astype(F32)
        squares = squares + jnp.sum(part * part, axis=1, keepdims=True)
    inverse = lax.rsqrt(squares / D + 1e-05)
    for s in range(8):
        cols = slice(256 * (s % 2), 256 * (s % 2) + 256)
        part = hbuf[s // 2, :, cols].astype(F32) + obuf[s].astype(F32)
        unit = (part * inverse * gbuf[s // 2, 0:1, cols]).astype(BF16)
        sent = jnp.dot(disp[...], unit, preferred_element_type=F32)
        for c in range(2):
            rows32[pl.ds(2 * s + c, 192, stride=16), :] = sent[:, 128 * c : 128 * (c + 1)]
    for b in range(8):
        dsend[pl.ds(8 * b, 8)] = rows32[pl.ds(384 * b, 384), :].astype(BF16).reshape(8, 48, 128)

    steps = ((3, 5), (2, 6), (4, 0), (1, 7))

    def near(g, m, sign):
        low, high = steps[g]
        x = lax.rem(mx + m, 2)
        y = lax.rem(my + 8 + sign * (low + (high - low) * (m // 2)), 8)
        return x * 64 + y * 8

    def send_rows(g, m, kinds):
        column_ = near(g, m, 1)
        for off, member, slot_ in (
            (2, 1 - i, 3),
            (1, 0, 1 + i),
            (3, 1, 1 + i),
            (0, i, 0),
        )[kinds]:
            pair = lax.rem(zp + off, 4)
            remote(
                dsend.at[column_ // 2 + pair],
                drecv.at[1, 16 * g + 4 * m + slot_],
                ds_sem.at[g],
                d_sem.at[g],
                column_ + 2 * pair + member,
                f,
            ).start()

    def send_group(g, each):
        def one(m, carry):
            each(g, m, slice(0, 4))
            return carry

        if 0 in steps[g]:
            lax.fori_loop(0, 2, one, 0)
            each(g, 2, slice(0, 3))
            each(g, 3, slice(0, 4))
        else:
            lax.fori_loop(0, 4, one, 0)

    own_d = pltpu.make_async_copy(dsend.at[me // 2], drecv.at[1, OWN], d_sem.at[OWN // 16])
    own_d.start()
    send_group(0, send_rows)
    send_group(1, send_rows)
    send_group(2, send_rows)
    send_group(3, send_rows)
    for g in range(4):
        span = pl.ds(16 * g, 16)
        wait(drecv.at[1, span], d_sem.at[g])
        remote(drecv.at[1, span], drecv.at[0, span], FS, fwd_sem.at[g], nb, f).start()

    wait(wg.at[early], sems.at[UX])
    remote(wu.at[shard(f2, 0, 176)], wu.at[shard(f2, 0, 176)], UFS, sems.at[UF], me, f1).start()
    wait(wg.at[pl.ds(0, 528)], sems.at[LOCW])
    wait(wg.at[early], sems.at[WC])
    wait(wg.at[early], sems.at[WF])
    wait(wg.at[early], sems.at[UC])
    wait(wg.at[early], sems.at[UF])

    def hidden(part_, kind, first_slot, rows, mine_buf):
        def widen(b, carry):
            wide32[pl.ds(pl.multiple_of(384 * b, 384), 384), :] = (
                drecv[kind, pl.ds(pl.multiple_of(first_slot + 8 * b, 8), 8)].reshape(384, 128).astype(F32)
            )
            return carry

        lax.fori_loop(0, rows // 24, widen, 0)
        for c in range(16):
            xbuf[0:rows, 128 * c : 128 * (c + 1)] = wide32[pl.ds(c, rows, stride=16), :].astype(BF16)
        x = xbuf[0:rows, :]
        for lo, hi in ((0, 256), (256, 512), (512, 704)):
            gate = lax.dot_general(x, wg[lo:hi, :], NT, preferred_element_type=F32)
            up = lax.dot_general(x, wu[lo:hi, :], NT, preferred_element_type=F32)
            mine_buf[f, :, lo:hi] = (gate / (1.0 + jnp.exp(-gate)) * up).astype(BF16)
        here = mine_buf.at[f]
        remote(here, here, AS + 3 * part_, a_sem.at[part_, 0], me, f2).start()
        remote(here, here, AS + 3 * part_ + 1, a_sem.at[part_, 1], me, f1).start()

    def share_on(part_, buf):
        wait(buf.at[0], a_sem.at[part_, 0])
        remote(buf.at[f2], buf.at[f2], AS + 3 * part_ + 2, a_sem.at[part_, 2], me, f1).start()

    def lower(part_, buf, rows, out32):
        for s in (1, 2):
            wait(buf.at[0], a_sem.at[part_, s])
        for g in range(4):
            out = jnp.dot(buf[g], wd[...], preferred_element_type=F32)
            for c in range(4):
                out32[pl.ds(4 * g + c, rows, stride=16), :] = out[:, 128 * c : 128 * (c + 1)]

    def partner(g):
        span = pl.ds(16 * g, 16)
        psend[span] = part32[...].astype(BF16).reshape(16, 48, 128)
        remote(psend.at[span], precv.at[span], PS, p_sem.at[g], nb, f).start()

    def send_back(g, m, kinds):
        column_ = near(g, m, -1)
        side = 2 * lax.rem(zp + 3 + 2 * i, 4)
        for slot_, z in ((3, 2 * lax.rem(zp + 2, 4) + 1 - i), (1, side), (2, side + 1), (0, mz))[kinds]:
            remote(
                rsend.at[16 * g + 4 * m + slot_], rrecv.at[me // 2], RS, sems.at[RR], column_ + z, f
            ).start()

    def give_back(g):
        span = pl.ds(16 * g, 16)
        wait(precv.at[span], p_sem.at[g])
        own = rows32[768 * g : 768 * (g + 1), :].astype(BF16).astype(F32)
        other = precv[span].reshape(768, 128).astype(F32)
        rsend[span] = (own + other).astype(BF16).reshape(16, 48, 128)
        if g == OWN // 16:
            own_r = pltpu.make_async_copy(rsend.at[OWN], rrecv.at[me // 2], sems.at[RR])
            own_r.start()
        send_group(g, send_back)

    parts = [abuf_b.at[g] for g in range(4)]
    hidden(0, 1, 0, 192, abuf_a)
    for g in range(4):
        wait(drecv.at[0, pl.ds(0, 16)], fwd_sem.at[g])
        if g > 0:
            share_on(g, parts[g - 1])
        hidden(g + 1, 0, 16 * g, 48, parts[g])
        if g == 0:
            share_on(0, abuf_a)
        else:
            lower(g, parts[g - 1], 48, part32)
            partner(g - 1)
        if g == 1:
            lower(0, abuf_a, 192, rows32)
    give_back(0)
    share_on(4, parts[3])
    lower(4, parts[3], 48, part32)
    partner(3)
    for g in range(1, 4):
        give_back(g)
    wait(rrecv, sems.at[RR])

    def widen_back(b, carry):
        rows32[pl.ds(pl.multiple_of(384 * b, 384), 384), :] = (
            rrecv[pl.ds(pl.multiple_of(8 * b, 8), 8)].reshape(384, 128).astype(F32)
        )
        return carry

    lax.fori_loop(0, 8, widen_back, 0)
    for c in range(4):
        ybuf[:, 128 * c : 128 * (c + 1)] = rows32[pl.ds(c, 768, stride=4), :].astype(BF16)
    total = jnp.dot(comb_hi[...], ybuf[...], preferred_element_type=F32)
    total = total + jnp.dot(comb_lo[...], ybuf[...], preferred_element_type=F32)
    for s in range(2):
        cols = slice(256 * s, 256 * (s + 1))
        mine_o = obuf[2 * f + s]
        att_ref[:, cols] = mine_o
        summed = hbuf[f, :, cols].astype(F32) + mine_o.astype(F32)
        mix_ref[:, cols] = (summed + total[:, cols]).astype(BF16)

    wait(qsend, sems.at[QS])
    wait(kvr_a.at[pl.ds(0, 15)], sems.at[K1])
    wait(kvr_a.at[pl.ds(0, 15)], sems.at[K2])
    wait(kvr_b.at[pl.ds(0, 7)], sems.at[K3])
    wait(kvr_b.at[pl.ds(0, 7)], sems.at[K4])
    wait(hbuf.at[pl.ds(0, 2)], sems.at[HS])
    wait(hbuf.at[0], sems.at[HFS])
    wait(gbuf.at[pl.ds(0, 3)], sems.at[GS])
    wait(obuf.at[pl.ds(0, 4)], sems.at[OS])
    wait(obuf.at[pl.ds(0, 3)], sems.at[OFS])
    wait(rrecv.at[pl.ds(0, 16)], ds_sem.at[0])
    wait(rrecv.at[pl.ds(0, 16)], ds_sem.at[1])
    wait(rrecv.at[pl.ds(0, 15)], ds_sem.at[2])
    wait(rrecv.at[pl.ds(0, 16)], ds_sem.at[3])
    wait(drecv.at[0], sems.at[FS])
    wait(precv, sems.at[PS])
    wait(rrecv.at[pl.ds(0, 63)], sems.at[RS])
    for s in (WS, WT, WFS):
        wait(wg.at[early], sems.at[s])
    for s in (US, UT, UFS):
        wait(wg.at[early], sems.at[s])
    for s in range(3):
        wait(abuf_a.at[0], sems.at[AS + s])
        for part_ in range(1, 5):
            wait(abuf_b.at[0, 0], sems.at[AS + 3 * part_ + s])


def per_device(
    hidden_state_stream,
    question_vectors,
    memory_lookup_vectors,
    content_vectors,
    logit_multiplier,
    chosen_tile_lists,
    premix_rmsnorm_scaling,
    routing_choice_ids,
    routing_shares,
    gating_matrix,
    raising_matrix,
    lowering_matrix,
):
    src = (chosen_tile_lists[:, :, None] * 4 + jnp.arange(4, dtype=jnp.int32)).reshape(1, 1024)
    vmem = pl.BlockSpec(memory_space=pltpu.VMEM)
    hbm = pl.BlockSpec(memory_space=pl.ANY)
    scratch = [
        pltpu.VMEM((16, 4, 2, 2, 32, 128), BF16),
        pltpu.VMEM((8, 16, 32, 128), BF16),
        pltpu.VMEM((16, 4, 2, 32, 128), BF16),
        pltpu.VMEM((16, 8, 32, 128), BF16),
        pltpu.VMEM((8, 16, 32, 128), BF16),
        pltpu.VMEM((256, 512), BF16),
        pltpu.VMEM((2, 256, 256), BF16),
        pltpu.VMEM((256, 256), BF16),
        pltpu.VMEM((4, 256, 512), BF16),
        pltpu.VMEM((4, 1, 512), F32),
        pltpu.VMEM((8, 256, 256), BF16),
        pltpu.VMEM((2, 256, 256), BF16),
        pltpu.VMEM((2, 2, 256, 128), F32),
        pltpu.VMEM((2, 2, 256, 128), F32),
        pltpu.VMEM((192, 256), BF16),
        pltpu.VMEM((256, 768), BF16),
        pltpu.VMEM((256, 768), BF16),
        pltpu.VMEM((3072, 128), F32),
        pltpu.VMEM((768, 128), F32),
        pltpu.VMEM((3072, 128), F32),
        pltpu.VMEM((64, 48, 128), BF16),
        pltpu.VMEM((2, 64, 48, 128), BF16),
        pltpu.VMEM((192, 2048), BF16),
        pltpu.VMEM((4, 192, 704), BF16),
        pltpu.VMEM((4, 4, 48, 704), BF16),
        pltpu.VMEM((64, 48, 128), BF16),
        pltpu.VMEM((64, 48, 128), BF16),
        pltpu.VMEM((64, 48, 128), BF16),
        pltpu.VMEM((64, 48, 128), BF16),
        pltpu.VMEM((768, 512), BF16),
        pltpu.VMEM((704, 2048), BF16),
        pltpu.VMEM((704, 2048), BF16),
        pltpu.VMEM((704, 512), BF16),
        pltpu.SemaphoreType.DMA((56,)),
        pltpu.SemaphoreType.DMA((4,)),
        pltpu.SemaphoreType.DMA((4,)),
        pltpu.SemaphoreType.DMA((4,)),
        pltpu.SemaphoreType.DMA((4,)),
        pltpu.SemaphoreType.DMA((4,)),
        pltpu.SemaphoreType.DMA((4,)),
        pltpu.SemaphoreType.DMA((5, 3)),
        pltpu.SemaphoreType.DMA((2,)),
    ]
    shape = jax.ShapeDtypeStruct((256, 512), BF16)
    return pl.pallas_call(
        layer_kernel,
        out_shape=(shape, shape),
        in_specs=[pl.BlockSpec(memory_space=pltpu.SMEM)] + [hbm] * 2 + [vmem] * 6 + [hbm] * 3,
        out_specs=(vmem, vmem),
        scratch_shapes=scratch,
        name="layer",
        cost_estimate=pl.CostEstimate(flops=5_000_000_000, bytes_accessed=20_000_000, transcendentals=3_000_000),
        compiler_params=pltpu.CompilerParams(
            collective_id=1, has_side_effects=True, vmem_limit_bytes=52 * 2**20
        ),
    )(
        logit_multiplier,
        hidden_state_stream,
        question_vectors,
        memory_lookup_vectors.reshape(256, 512),
        content_vectors.reshape(256, 512),
        src,
        premix_rmsnorm_scaling[None, :],
        routing_choice_ids.T,
        routing_shares.T,
        gating_matrix,
        raising_matrix,
        lowering_matrix,
    )


def solution(mesh):
    in_specs = (
        P("ctx", "exp"),
        P("ctx", "exp"),
        P(None, "ctx", "exp"),
        P(None, "ctx", "exp"),
        P("exp"),
        P(),
        P("exp"),
        P("ctx", None),
        P("ctx", None),
        P("ctx", "exp", None),
        P("ctx", "exp", None),
        P("ctx", None, "exp"),
    )
    out_specs = (P("ctx", "exp"), P("ctx", "exp"))
    return jax.shard_map(
        per_device, mesh=mesh, in_specs=in_specs, out_specs=out_specs, check_vma=False
    )
```

```python
import functools
import math

import jax
import jax.numpy as jnp
from jax import lax
from jax.experimental import pallas as pl
from jax.experimental.pallas import tpu as pltpu
from jax.sharding import PartitionSpec as P

D = 2048
EXPERTS = 64
CAP = 12
N = 128
OWN = 40
MESH = pl.DeviceIdType.MESH
F32 = jnp.float32
BF16 = jnp.bfloat16

NT = (((1,), (1,)), ((), ()))


def unit_heads(x):
    parts = []
    for h in range(x.shape[1] // 128):
        s = x[:, 128 * h : 128 * (h + 1)].astype(F32)
        parts.append(s * lax.rsqrt(jnp.mean(s * s, axis=1, keepdims=True) + 1e-06))
    return jnp.concatenate(parts, axis=1).astype(BF16)


def layer_kernel(
    mult_ref,
    hid_ref,
    q_ref,
    k_ref,
    v_ref,
    src_ref,
    gain_ref,
    ids_ref,
    share_ref,
    gate_ref,
    up_ref,
    down_ref,
    att_ref,
    mix_ref,
    kvs,
    mid_a,
    mid_b,
    kvr_a,
    kvr_b,
    qown,
    qbuf,
    qsend,
    hbuf,
    gbuf,
    obuf,
    osend,
    acc,
    den,
    disp,
    comb_hi,
    comb_lo,
    rows32,
    part32,
    wide32,
    dsend,
    drecv,
    xbuf,
    abuf_a,
    abuf_b,
    psend,
    precv,
    rsend,
    rrecv,
    ybuf,
    wg,
    wu,
    wd,
    sems,
    kva_sem,
    kvb_sem,
    d_sem,
    ds_sem,
    fwd_sem,
    p_sem,
    a_sem,
    in_sem,
):
    me = lax.axis_index("ctx")
    f = lax.axis_index("exp")
    i = lax.rem(me, 2)
    nb = me + 1 - 2 * i
    f1 = f + 1 - 2 * lax.rem(f, 2)
    f2 = lax.rem(f + 2, 4)
    f3 = 3 - f
    mz = lax.rem(me, 8)
    my = lax.rem(me // 8, 8)
    mx = me // 64
    zp = mz // 2
    xy = me // 8
    (QS, QR, HS, HX, HC, HF, HFS, GS, GR, OS, OR, DS, FS, PS, RS, RR, OX, OY, OZ, OFS, K1, K2, K3, K4, KA, KB, KL, KM) = range(16 + 12)
    (WS, WX, WT, WC, WF, WFS, US, UX, UT, UC, UF, UFS, LOCW) = range(28, 41)
    AS = 41

    own_q = pltpu.make_async_copy(q_ref, qown, in_sem.at[0])
    own_q.start()
    own_h = pltpu.make_async_copy(hid_ref, hbuf.at[f], in_sem.at[1])
    own_h.start()

    bar = pltpu.get_barrier_semaphore()

    def hail(k, offs):
        for off in offs:
            to = lax.rem(xy + k, 16) * 8 + lax.rem(mz + 8 + off, 8)
            pl.semaphore_signal(bar, inc=1, device_id=(to, f), device_id_type=MESH)

    def greet(k, carry):
        hail(k, (0, 2, -2, 2 * i - 1, 6 * i - 3))
        return carry

    hail(0, (1, 2, 3, 4, 5, 6, 7))
    lax.fori_loop(1, 16, greet, 0)
    for g in (f1, f2, f3):
        pl.semaphore_signal(bar, inc=1, device_id=(me, g), device_id_type=MESH)
        pl.semaphore_signal(bar, inc=1, device_id=(nb, g), device_id_type=MESH)

    pick = (lax.broadcasted_iota(jnp.int32, (256, 1024), 0) == src_ref[...]).astype(F32)
    pick = jnp.transpose(pick).astype(BF16)
    kunit = unit_heads(k_ref[...])
    for half in range(2):
        for head in range(2):
            cols = slice(256 * half + 128 * head, 256 * half + 128 * head + 128)
            got = jnp.dot(pick, kunit[:, cols], preferred_element_type=F32).astype(BF16)
            kvs[:, :, half, head, 0:16, :] = got.reshape(16, 4, 16, 128)
            got = jnp.dot(pick, v_ref[:, cols], preferred_element_type=F32).astype(BF16)
            kvs[:, :, half, head, 16:32, :] = got.reshape(16, 4, 16, 128)

    pl.semaphore_wait(bar, 7 + 15 * 5 + 6)

    def remote(src, dst, s, r, ctx, ex):
        left = sems.at[s] if isinstance(s, int) else s
        return pltpu.make_async_remote_copy(
            src, dst, left, r, device_id=(ctx, ex), device_id_type=MESH
        )

    def wait(ref, sem):
        pltpu.make_async_copy(ref, ref, sem).wait()

    def ring(k):
        return xy * 8 + lax.rem(mz + k, 8)

    def column(k):
        return lax.rem(xy + k, 16) * 8 + mz

    def first_z(k):
        d = lax.rem(mz + k, 8)
        src = kvs.at[:, d // 2, lax.rem(d, 2), 0]
        remote(src, mid_a.at[mz], K3, sems.at[KA], ring(k), f).start()

    def first_xy(k):
        d = lax.rem(xy + k, 16)
        remote(kvs.at[d, :, :, 1], mid_b.at[xy], K1, sems.at[KB], column(k), f).start()

    def first_step(k, carry):
        first_z(k)
        first_xy(2 * k - 1)
        first_xy(2 * k)
        return carry

    lax.fori_loop(1, 8, first_step, 0)
    first_xy(15)
    own_a = pltpu.make_async_copy(kvs.at[:, mz // 2, lax.rem(mz, 2), 0], mid_a.at[mz], sems.at[KM])
    own_a.start()
    own_b = pltpu.make_async_copy(kvs.at[xy, :, :, 1], mid_b.at[xy], sems.at[KL])
    own_b.start()

    def shard(who, lo, hi):
        return pl.ds(pl.multiple_of(who * 176 + lo, 16), hi - lo)

    for g, left, sem in ((f2, WS, WX), (f1, WT, WC)):
        remote(gate_ref.at[0], wg.at[shard(f, 0, 176)], left, sems.at[sem], me, g).start()
    for c in (
        pltpu.make_async_copy(gate_ref.at[0], wg.at[shard(f, 0, 176)], sems.at[LOCW]),
        pltpu.make_async_copy(up_ref.at[0], wu.at[shard(f, 0, 176)], sems.at[LOCW]),
        pltpu.make_async_copy(down_ref.at[0], wd, sems.at[LOCW]),
    ):
        c.start()

    own_q.wait()
    own_h.wait()
    qunit = unit_heads(qown[...])
    first = jnp.broadcast_to(i, (256, 256)) == 0
    qbuf[i] = jnp.where(first, qunit[:, :256], qunit[:, 256:])
    qsend[...] = jnp.where(first, qunit[:, 256:], qunit[:, :256])
    remote(qsend, qbuf.at[i], QS, sems.at[QR], nb, f).start()

    for g, sem in ((f2, HX), (f1, HC)):
        remote(hbuf.at[f], hbuf.at[f], HS, sems.at[sem], me, g).start()
    for g in (f1, f2, f3):
        remote(gain_ref, gbuf.at[f], GS, sems.at[GR], me, g).start()
    gbuf[f] = gain_ref[...]

    ids = ids_ref[...]
    experts = lax.broadcasted_iota(jnp.int32, (EXPERTS, 256), 0)
    named = [(experts == ids[c : c + 1, :]).astype(F32) for c in range(2)]
    counts = (named[0] + named[1]).astype(BF16)
    earlier = (
        lax.broadcasted_iota(jnp.int32, (256, 256), 0) < lax.broadcasted_iota(jnp.int32, (256, 256), 1)
    ).astype(F32).astype(BF16)
    before = jnp.dot(counts, earlier, preferred_element_type=F32)
    keys = []
    for c in range(2):
        rank = jnp.sum(named[c] * before, axis=0, keepdims=True)
        keys.append(ids[c : c + 1, :] * CAP + rank.astype(jnp.int32))
    row = lax.broadcasted_iota(jnp.int32, (192, 256), 0)
    expert = (row * 171) // 512
    slot = expert * CAP + (row - expert * 3)
    mine = slot + 3 * f
    disp[...] = ((keys[0] == mine) | (keys[1] == mine)).astype(F32).astype(BF16)
    for b in range(3):
        line = lax.broadcasted_iota(jnp.int32, (256, 256), 0) + 256 * b
        expert = (line * 5462) // 65536
        inner = line - expert * 12
        there = expert * CAP + 3 * lax.rem(inner, 4) + inner // 4
        table = jnp.where(keys[0] == there, share_ref[0:1, :], 0.0) + jnp.where(
            keys[1] == there, share_ref[1:2, :], 0.0
        )
        high = table.astype(BF16).astype(F32)
        comb_hi[:, 256 * b : 256 * (b + 1)] = jnp.transpose(high).astype(BF16)
        comb_lo[:, 256 * b : 256 * (b + 1)] = jnp.transpose(table - high).astype(BF16)

    own_a.wait()
    own_b.wait()
    wait(mid_a.at[pl.ds(0, 7)], sems.at[KA])
    own_a = pltpu.make_async_copy(mid_a.at[:, xy], kvr_a.at[0], kva_sem.at[0])
    own_a.start()

    def second_xy(k, carry):
        d = lax.rem(xy + k, 16)
        remote(mid_a.at[:, d], kvr_a.at[k], K2, kva_sem.at[k // 4], column(k), f).start()
        return carry

    lax.fori_loop(1, 16, second_xy, 0)
    wait(mid_b.at[pl.ds(0, 15)], sems.at[KB])
    own_b = pltpu.make_async_copy(mid_b.at[:, mz // 2, lax.rem(mz, 2)], kvr_b.at[0], kvb_sem.at[0])
    own_b.start()

    def second_z(k, carry):
        d = lax.rem(mz + k, 8)
        remote(
            mid_b.at[:, d // 2, lax.rem(d, 2)], kvr_b.at[k], K4, kvb_sem.at[k // 2], ring(k), f
        ).start()
        return carry

    lax.fori_loop(1, 8, second_z, 0)

    acc[...] = jnp.zeros_like(acc)
    den[...] = jnp.zeros_like(den)
    wait(qbuf.at[0], sems.at[QR])

    def attend(h, kg, vg):
        cols = slice(128 * h, 128 * (h + 1))
        scale = mult_ref[2 * i + h] * (1.0 / math.sqrt(128.0))
        for j in range(2):
            s = lax.dot_general(qbuf[j, :, cols], kg, NT, preferred_element_type=F32)
            e = jnp.exp(s * scale)
            total = e[:, 0:128]
            for c in range(1, 4):
                total = total + e[:, 128 * c : 128 * (c + 1)]
            den[j, h] += total
            acc[j, h] += jnp.dot(e.astype(BF16), vg, preferred_element_type=F32)

    def attend_group(g, carry):
        wait(kvr_a.at[pl.ds(0, 4)], kva_sem.at[g])
        span = pl.ds(pl.multiple_of(4 * g, 4), 4)
        attend(0, kvr_a[span, :, 0:16, :].reshape(512, 128), kvr_a[span, :, 16:32, :].reshape(512, 128))
        wait(kvr_b.at[pl.ds(0, 2)], kvb_sem.at[g])
        span = pl.ds(pl.multiple_of(2 * g, 2), 2)
        attend(1, kvr_b[span, :, 0:16, :].reshape(512, 128), kvr_b[span, :, 16:32, :].reshape(512, 128))
        return carry

    lax.fori_loop(0, 4, attend_group, 0)
    for j in range(2):
        for h in range(2):
            out = acc[j, h] / jnp.sum(den[j, h], axis=1, keepdims=True)
            osend[j, :, 128 * h : 128 * (h + 1)] = out.astype(BF16)

    wait(hbuf.at[0], sems.at[HX])
    remote(hbuf.at[f2], hbuf.at[f2], HFS, sems.at[HF], me, f1).start()
    mark = 2 * f + i
    for src, ctx, sem in ((i, me, OX), (1 - i, nb, OY)):
        remote(osend.at[src], obuf.at[mark], OS, sems.at[sem], ctx, f2).start()
    remote(osend.at[1 - i], obuf.at[mark], OS, sems.at[OZ], nb, f).start()
    remote(osend.at[i], obuf.at[mark], OS, sems.at[OR], me, f1).start()
    obuf[mark] = osend[i]
    for who, sem in ((2 * f + 1 - i, OZ), (2 * f2 + i, OX), (2 * f2 + 1 - i, OY)):
        wait(obuf.at[0], sems.at[sem])
        remote(obuf.at[who], obuf.at[who], OFS, sems.at[OR], me, f1).start()
    early = pl.ds(0, 176)
    wait(wg.at[early], sems.at[WX])
    remote(wg.at[shard(f2, 0, 176)], wg.at[shard(f2, 0, 176)], WFS, sems.at[WF], me, f1).start()
    wait(hbuf.at[0], sems.at[HC])
    wait(hbuf.at[0], sems.at[HF])
    wait(gbuf.at[pl.ds(0, 3)], sems.at[GR])
    wait(obuf.at[pl.ds(0, 4)], sems.at[OR])

    for g, left, sem in ((f2, US, UX), (f1, UT, UC)):
        remote(up_ref.at[0], wu.at[shard(f, 0, 176)], left, sems.at[sem], me, g).start()

    squares = jnp.zeros((256, 1), F32)
    for s in range(8):
        cols = slice(256 * (s % 2), 256 * (s % 2) + 256)
        part = hbuf[s // 2, :, cols].astype(F32) + obuf[s].astype(F32)
        squares = squares + jnp.sum(part * part, axis=1, keepdims=True)
    inverse = lax.rsqrt(squares / D + 1e-05)
    for s in range(8):
        cols = slice(256 * (s % 2), 256 * (s % 2) + 256)
        part = hbuf[s // 2, :, cols].astype(F32) + obuf[s].astype(F32)
        unit = (part * inverse * gbuf[s // 2, 0:1, cols]).astype(BF16)
        sent = jnp.dot(disp[...], unit, preferred_element_type=F32)
        for c in range(2):
            rows32[pl.ds(2 * s + c, 192, stride=16), :] = sent[:, 128 * c : 128 * (c + 1)]
    for b in range(8):
        dsend[pl.ds(8 * b, 8)] = rows32[pl.ds(384 * b, 384), :].astype(BF16).reshape(8, 48, 128)

    steps = ((3, 5), (2, 6), (4, 0), (1, 7))

    def near(g, m, sign):
        low, high = steps[g]
        x = lax.rem(mx + m, 2)
        y = lax.rem(my + 8 + sign * (low + (high - low) * (m // 2)), 8)
        return x * 64 + y * 8

    def send_rows(g, m, kinds):
        column_ = near(g, m, 1)
        for off, member, slot_ in (
            (2, 1 - i, 3),
            (1, 0, 1 + i),
            (3, 1, 1 + i),
            (0, i, 0),
        )[kinds]:
            pair = lax.rem(zp + off, 4)
            remote(
                dsend.at[column_ // 2 + pair],
                drecv.at[1, 16 * g + 4 * m + slot_],
                ds_sem.at[g],
                d_sem.at[g],
                column_ + 2 * pair + member,
                f,
            ).start()

    def send_group(g, each):
        def one(m, carry):
            each(g, m, slice(0, 4))
            return carry

        if 0 in steps[g]:
            lax.fori_loop(0, 2, one, 0)
            each(g, 2, slice(0, 3))
            each(g, 3, slice(0, 4))
        else:
            lax.fori_loop(0, 4, one, 0)

    own_d = pltpu.make_async_copy(dsend.at[me // 2], drecv.at[1, OWN], d_sem.at[OWN // 16])
    own_d.start()
    send_group(0, send_rows)
    send_group(1, send_rows)
    send_group(2, send_rows)
    send_group(3, send_rows)
    for g in range(4):
        span = pl.ds(16 * g, 16)
        wait(drecv.at[1, span], d_sem.at[g])
        remote(drecv.at[1, span], drecv.at[0, span], FS, fwd_sem.at[g], nb, f).start()

    wait(wg.at[early], sems.at[UX])
    remote(wu.at[shard(f2, 0, 176)], wu.at[shard(f2, 0, 176)], UFS, sems.at[UF], me, f1).start()
    wait(wg.at[pl.ds(0, 528)], sems.at[LOCW])
    wait(wg.at[early], sems.at[WC])
    wait(wg.at[early], sems.at[WF])
    wait(wg.at[early], sems.at[UC])
    wait(wg.at[early], sems.at[UF])

    def hidden(part_, kind, first_slot, rows, mine_buf):
        def widen(b, carry):
            wide32[pl.ds(pl.multiple_of(384 * b, 384), 384), :] = (
                drecv[kind, pl.ds(pl.multiple_of(first_slot + 8 * b, 8), 8)].reshape(384, 128).astype(F32)
            )
            return carry

        lax.fori_loop(0, rows // 24, widen, 0)
        for c in range(16):
            xbuf[0:rows, 128 * c : 128 * (c + 1)] = wide32[pl.ds(c, rows, stride=16), :].astype(BF16)
        x = xbuf[0:rows, :]
        for lo, hi in ((0, 256), (256, 512), (512, 704)):
            gate = lax.dot_general(x, wg[lo:hi, :], NT, preferred_element_type=F32)
            up = lax.dot_general(x, wu[lo:hi, :], NT, preferred_element_type=F32)
            mine_buf[f, :, lo:hi] = (gate / (1.0 + jnp.exp(-gate)) * up).astype(BF16)
        here = mine_buf.at[f]
        remote(here, here, AS + 3 * part_, a_sem.at[part_, 0], me, f2).start()
        remote(here, here, AS + 3 * part_ + 1, a_sem.at[part_, 1], me, f1).start()

    def share_on(part_, buf):
        wait(buf.at[0], a_sem.at[part_, 0])
        remote(buf.at[f2], buf.at[f2], AS + 3 * part_ + 2, a_sem.at[part_, 2], me, f1).start()

    def lower(part_, buf, rows, out32):
        for s in (1, 2):
            wait(buf.at[0], a_sem.at[part_, s])
        for g in range(4):
            out = jnp.dot(buf[g], wd[...], preferred_element_type=F32)
            for c in range(4):
                out32[pl.ds(4 * g + c, rows, stride=16), :] = out[:, 128 * c : 128 * (c + 1)]

    def partner(g):
        span = pl.ds(16 * g, 16)
        psend[span] = part32[...].astype(BF16).reshape(16, 48, 128)
        remote(psend.at[span], precv.at[span], PS, p_sem.at[g], nb, f).start()

    def send_back(g, m, kinds):
        column_ = near(g, m, -1)
        side = 2 * lax.rem(zp + 3 + 2 * i, 4)
        for slot_, z in ((3, 2 * lax.rem(zp + 2, 4) + 1 - i), (1, side), (2, side + 1), (0, mz))[kinds]:
            remote(
                rsend.at[16 * g + 4 * m + slot_], rrecv.at[me // 2], RS, sems.at[RR], column_ + z, f
            ).start()

    def give_back(g):
        span = pl.ds(16 * g, 16)
        wait(precv.at[span], p_sem.at[g])
        own = rows32[768 * g : 768 * (g + 1), :].astype(BF16).astype(F32)
        other = precv[span].reshape(768, 128).astype(F32)
        rsend[span] = (own + other).astype(BF16).reshape(16, 48, 128)
        if g == OWN // 16:
            own_r = pltpu.make_async_copy(rsend.at[OWN], rrecv.at[me // 2], sems.at[RR])
            own_r.start()
        send_group(g, send_back)

    parts = [abuf_b.at[g] for g in range(4)]
    hidden(0, 1, 0, 192, abuf_a)
    for g in range(4):
        wait(drecv.at[0, pl.ds(0, 16)], fwd_sem.at[g])
        if g > 0:
            share_on(g, parts[g - 1])
        hidden(g + 1, 0, 16 * g, 48, parts[g])
        if g == 0:
            share_on(0, abuf_a)
        else:
            lower(g, parts[g - 1], 48, part32)
            partner(g - 1)
        if g == 1:
            lower(0, abuf_a, 192, rows32)
    give_back(0)
    share_on(4, parts[3])
    lower(4, parts[3], 48, part32)
    partner(3)
    for g in range(1, 4):
        give_back(g)
    wait(rrecv, sems.at[RR])

    def widen_back(b, carry):
        rows32[pl.ds(pl.multiple_of(384 * b, 384), 384), :] = (
            rrecv[pl.ds(pl.multiple_of(8 * b, 8), 8)].reshape(384, 128).astype(F32)
        )
        return carry

    lax.fori_loop(0, 8, widen_back, 0)
    for c in range(4):
        ybuf[:, 128 * c : 128 * (c + 1)] = rows32[pl.ds(c, 768, stride=4), :].astype(BF16)
    total = jnp.dot(comb_hi[...], ybuf[...], preferred_element_type=F32)
    total = total + jnp.dot(comb_lo[...], ybuf[...], preferred_element_type=F32)
    for s in range(2):
        cols = slice(256 * s, 256 * (s + 1))
        mine_o = obuf[2 * f + s]
        att_ref[:, cols] = mine_o
        summed = hbuf[f, :, cols].astype(F32) + mine_o.astype(F32)
        mix_ref[:, cols] = (summed + total[:, cols]).astype(BF16)

    wait(qsend, sems.at[QS])
    wait(kvr_a.at[pl.ds(0, 15)], sems.at[K1])
    wait(kvr_a.at[pl.ds(0, 15)], sems.at[K2])
    wait(kvr_b.at[pl.ds(0, 7)], sems.at[K3])
    wait(kvr_b.at[pl.ds(0, 7)], sems.at[K4])
    wait(hbuf.at[pl.ds(0, 2)], sems.at[HS])
    wait(hbuf.at[0], sems.at[HFS])
    wait(gbuf.at[pl.ds(0, 3)], sems.at[GS])
    wait(obuf.at[pl.ds(0, 4)], sems.at[OS])
    wait(obuf.at[pl.ds(0, 3)], sems.at[OFS])
    wait(rrecv.at[pl.ds(0, 16)], ds_sem.at[0])
    wait(rrecv.at[pl.ds(0, 16)], ds_sem.at[1])
    wait(rrecv.at[pl.ds(0, 15)], ds_sem.at[2])
    wait(rrecv.at[pl.ds(0, 16)], ds_sem.at[3])
    wait(drecv.at[0], sems.at[FS])
    wait(precv, sems.at[PS])
    wait(rrecv.at[pl.ds(0, 63)], sems.at[RS])
    for s in (WS, WT, WFS):
        wait(wg.at[early], sems.at[s])
    for s in (US, UT, UFS):
        wait(wg.at[early], sems.at[s])
    for s in range(3):
        wait(abuf_a.at[0], sems.at[AS + s])
        for part_ in range(1, 5):
            wait(abuf_b.at[0, 0], sems.at[AS + 3 * part_ + s])


def per_device(
    hidden_state_stream,
    question_vectors,
    memory_lookup_vectors,
    content_vectors,
    logit_multiplier,
    chosen_tile_lists,
    premix_rmsnorm_scaling,
    routing_choice_ids,
    routing_shares,
    gating_matrix,
    raising_matrix,
    lowering_matrix,
):
    src = (chosen_tile_lists[:, :, None] * 4 + jnp.arange(4, dtype=jnp.int32)).reshape(1, 1024)
    vmem = pl.BlockSpec(memory_space=pltpu.VMEM)
    hbm = pl.BlockSpec(memory_space=pl.ANY)
    scratch = [
        pltpu.VMEM((16, 4, 2, 2, 32, 128), BF16),
        pltpu.VMEM((8, 16, 32, 128), BF16),
        pltpu.VMEM((16, 4, 2, 32, 128), BF16),
        pltpu.VMEM((16, 8, 32, 128), BF16),
        pltpu.VMEM((8, 16, 32, 128), BF16),
        pltpu.VMEM((256, 512), BF16),
        pltpu.VMEM((2, 256, 256), BF16),
        pltpu.VMEM((256, 256), BF16),
        pltpu.VMEM((4, 256, 512), BF16),
        pltpu.VMEM((4, 1, 512), F32),
        pltpu.VMEM((8, 256, 256), BF16),
        pltpu.VMEM((2, 256, 256), BF16),
        pltpu.VMEM((2, 2, 256, 128), F32),
        pltpu.VMEM((2, 2, 256, 128), F32),
        pltpu.VMEM((192, 256), BF16),
        pltpu.VMEM((256, 768), BF16),
        pltpu.VMEM((256, 768), BF16),
        pltpu.VMEM((3072, 128), F32),
        pltpu.VMEM((768, 128), F32),
        pltpu.VMEM((3072, 128), F32),
        pltpu.VMEM((64, 48, 128), BF16),
        pltpu.VMEM((2, 64, 48, 128), BF16),
        pltpu.VMEM((192, 2048), BF16),
        pltpu.VMEM((4, 192, 704), BF16),
        pltpu.VMEM((4, 4, 48, 704), BF16),
        pltpu.VMEM((64, 48, 128), BF16),
        pltpu.VMEM((64, 48, 128), BF16),
        pltpu.VMEM((64, 48, 128), BF16),
        pltpu.VMEM((64, 48, 128), BF16),
        pltpu.VMEM((768, 512), BF16),
        pltpu.VMEM((704, 2048), BF16),
        pltpu.VMEM((704, 2048), BF16),
        pltpu.VMEM((704, 512), BF16),
        pltpu.SemaphoreType.DMA((56,)),
        pltpu.SemaphoreType.DMA((4,)),
        pltpu.SemaphoreType.DMA((4,)),
        pltpu.SemaphoreType.DMA((4,)),
        pltpu.SemaphoreType.DMA((4,)),
        pltpu.SemaphoreType.DMA((4,)),
        pltpu.SemaphoreType.DMA((4,)),
        pltpu.SemaphoreType.DMA((5, 3)),
        pltpu.SemaphoreType.DMA((2,)),
    ]
    shape = jax.ShapeDtypeStruct((256, 512), BF16)
    return pl.pallas_call(
        layer_kernel,
        out_shape=(shape, shape),
        in_specs=[pl.BlockSpec(memory_space=pltpu.SMEM)] + [hbm] * 2 + [vmem] * 6 + [hbm] * 3,
        out_specs=(vmem, vmem),
        scratch_shapes=scratch,
        name="layer",
        cost_estimate=pl.CostEstimate(flops=5_000_000_000, bytes_accessed=20_000_000, transcendentals=3_000_000),
        compiler_params=pltpu.CompilerParams(
            collective_id=1, has_side_effects=True, vmem_limit_bytes=52 * 2**20
        ),
    )(
        logit_multiplier,
        hidden_state_stream,
        question_vectors,
        memory_lookup_vectors.reshape(256, 512),
        content_vectors.reshape(256, 512),
        src,
        premix_rmsnorm_scaling[None, :],
        routing_choice_ids.T,
        routing_shares.T,
        gating_matrix,
        raising_matrix,
        lowering_matrix,
    )


def solution(mesh):
    in_specs = (
        P("ctx", "exp"),
        P("ctx", "exp"),
        P(None, "ctx", "exp"),
        P(None, "ctx", "exp"),
        P("exp"),
        P(),
        P("exp"),
        P("ctx", None),
        P("ctx", None),
        P("ctx", "exp", None),
        P("ctx", "exp", None),
        P("ctx", None, "exp"),
    )
    out_specs = (P("ctx", "exp"), P("ctx", "exp"))
    return jax.shard_map(
        per_device, mesh=mesh, in_specs=in_specs, out_specs=out_specs, check_vma=False
    )
```
